32 devices in a mesh: head: 8 (over y, x, core), dp: 4 (over z).
Axes of the slice: x: 2, y: 2, z: 4, core: 2. Of those that a mesh axis runs over, the one named last changes fastest.
Arguments:
- layer_input: bfloat16 [8, 1024, 2048], P('dp', 'head'), may hold values from -6 to 6
- doc_starts: int32 [8, 1024], P('dp'), may hold values from 0 to 1, as said below
- norm1_gain: float32 [2048], replicated, may hold values from 0.5 to 1.5
- w_query: bfloat16 [2048, 2048], P(None, 'head'), may hold values from -0.125 to 0.125
- w_forget: bfloat16 [2048, 2048], P(None, 'head'), may hold values from -0.125 to 0.125
- w_input: bfloat16 [2048, 2048], P(None, 'head'), may hold values from -0.125 to 0.125
- w_gate_out: bfloat16 [2048, 2048], P(None, 'head'), may hold values from -0.125 to 0.125
- forget_floor: float32 [2048], P('head'), may hold values from 0.92 to 1
- group_gain: float32 [2048], P('head'), may hold values from 0.5 to 1.5
- w_out: bfloat16 [2048, 2048], P('head'), may hold values from -0.125 to 0.125
- norm2_gain: float32 [2048], replicated, may hold values from 0.5 to 1.5
- ffn_gate: bfloat16 [2048, 5632], P(None, ('head', 'dp')), may hold values from -0.125 to 0.125
- ffn_up: bfloat16 [2048, 5632], P(None, ('head', 'dp')), may hold values from -0.125 to 0.125
- ffn_down: bfloat16 [2048, 5632], P(None, ('head', 'dp')), may hold values from -0.078125 to 0.078125
- out_cotangent: bfloat16 [8, 1024, 2048], P('dp', 'head'), may hold values from -6 to 6
Outputs:
- output: bfloat16 [8, 1024, 2048], P('dp', 'head')
- input_grad: float32 [8, 1024, 2048], P('dp', 'head')
- query_grad: float32 [2048, 2048], P('dp', 'head')
- forget_grad: float32 [2048, 2048], P('dp', 'head')
- input_proj_grad: float32 [2048, 2048], P('dp', 'head')
- gate_out_grad: float32 [2048, 2048], P('dp', 'head')
- out_proj_grad: float32 [2048, 2048], P('head', 'dp')
- group_gain_grad: float32 [2048], P(('head', 'dp'))
- floor_grad: float32 [2048], P(('head', 'dp'))
- norm1_gain_grad: float32 [2048], replicated
- norm2_gain_grad: float32 [2048], replicated
- ffn_gate_grad: float32 [2048, 5632], P(None, ('head', 'dp'))
- ffn_up_grad: float32 [2048, 5632], P(None, ('head', 'dp'))
- ffn_down_grad: float32 [2048, 5632], P(None, ('head', 'dp'))
The draws below stay inside these ranges and needn't reach their ends.
Inputs may be any that keep to these rules, and one draw needn't show every extreme that they name: `doc_starts`: position 0 of every row is 1; every row has at most 4 other starts; in each aligned group of 2 rows one row, drawn from the seed, has exactly one other start, at a position below 64.
All inputs are finite; a program needn't handle non-finite values.
Results may differ from the reference program's by a relative error of at most 0.015.
The reference program's roundings to bfloat16 on the way count: a program that leaves them out, or rounds other values in their place, can miss the bound.
Values may be sent and summed in bfloat16 or wider, within the bound.
No kernel may reach another device: no remote copies, remote signals or barrier semaphores. Data moves between devices by JAX's collectives and lax.ppermute only.
A program may use at most 192 MiB of HBM per device.

```python
import math
import jax
import jax.numpy as jnp
from jax import lax

D = 2048
HEADS = 16
HEAD_DIM = 128
FF = 5632
LEN = 1024
ROWS_DEV = 2
ROWS = 8


def draw_doc_starts(key, part):
    key = jax.random.fold_in(key, 11)
    key_pos, key_count, key_pick, key_early = jax.random.split(key, 4)
    positions = jax.random.randint(key_pos, (ROWS, 4), 1, LEN)
    counts = jax.random.randint(key_count, (ROWS, 1), 1, 5)
    active = jnp.arange(4)[None, :] < counts
    marks = jnp.any((jnp.arange(LEN)[None, None, :] == positions[:, :, None]) & active[:, :, None], axis=1)
    picked = jax.random.randint(key_pick, (ROWS // ROWS_DEV,), 0, ROWS_DEV)
    clean = jnp.arange(ROWS) % ROWS_DEV == jnp.repeat(picked, ROWS_DEV)
    early = jax.random.randint(key_early, (ROWS, 1), 1, LEN // 16)
    early_marks = jnp.arange(LEN)[None, :] == early
    marks = jnp.where(clean[:, None], early_marks, marks)
    marks = marks | (jnp.arange(LEN)[None, :] == 0)
    return marks.astype(jnp.int32)


def draw_forget_floor(key, part):
    key = jax.random.fold_in(key, 7)
    key_kind, key_slow, key_fast = jax.random.split(key, 3)
    share = 0.5
    slow = jax.random.uniform(key_kind, (D,)) < share
    slow_gap = jnp.exp(jax.random.uniform(key_slow, (D,), jnp.float32, math.log(0.4 / LEN), math.log(3.0 / LEN)))
    fast_gap = jnp.exp(jax.random.uniform(key_fast, (D,), jnp.float32, math.log(0.02), math.log(0.08)))
    return (1.0 - jnp.where(slow, slow_gap, fast_gap)).astype(jnp.float32)


def block_levels(rng, extent, cuts, smallest, largest):
    level = 1.0
    for axis_at, blocks in cuts:
        steps = jax.random.uniform(jax.random.fold_in(jax.random.fold_in(rng, 6), axis_at), (blocks,), jnp.float32, smallest / len(cuts), largest / len(cuts))
        level = level * jnp.repeat(jnp.exp(steps), extent[axis_at] // blocks).reshape((-1,) + (1,) * (len(extent) - 1 - axis_at))
    return level


def centred(rng, extent, deviation, bound, shards=(), dtype=jnp.bfloat16):
    result = jax.random.normal(rng, extent, jnp.float32) * deviation
    if len(shards) > 0:
        result = block_levels(rng, extent, shards, -0.22, 0.18) * result
    return jnp.clip(result, min=-bound, max=bound).astype(dtype)


def setup_inputs(seed: int = 0) -> dict:
    key_list = jax.random.split(jax.random.key(seed), 16)
    layer_input = centred(key_list[0], (ROWS, LEN, D), 1.0, 6.0, ((0, 4), (1, 8)))
    doc_starts = draw_doc_starts(jax.random.fold_in(key_list[15], 71), 0)
    norm1_gain = jnp.clip(1.0 + 0.1 * jax.random.normal(key_list[2], (D,), jnp.float32), 0.5, 1.5)
    w_query = centred(key_list[3], (D, D), D ** -0.5, 0.125, ((1, 8),))
    w_forget = centred(key_list[4], (D, D), D ** -0.5, 0.125, ((1, 8),))
    w_input = centred(key_list[5], (D, D), D ** -0.5, 0.125, ((1, 8),))
    w_gate_out = centred(key_list[6], (D, D), D ** -0.5, 0.125, ((1, 8),))
    forget_floor = draw_forget_floor(jax.random.fold_in(key_list[15], 71), 0)
    group_gain = jnp.clip(1.0 + 0.1 * jax.random.normal(key_list[8], (D,), jnp.float32), 0.5, 1.5)
    w_out = centred(key_list[9], (D, D), D ** -0.5, 0.125, ((0, 8),))
    norm2_gain = jnp.clip(1.0 + 0.1 * jax.random.normal(key_list[10], (D,), jnp.float32), 0.5, 1.5)
    ffn_gate = centred(key_list[11], (D, FF), D ** -0.5, 0.125, ((1, 32),))
    ffn_up = centred(key_list[12], (D, FF), D ** -0.5, 0.125, ((1, 32),))
    ffn_down = centred(key_list[13], (D, FF), FF ** -0.5, 0.078125, ((1, 32),))
    out_cotangent = centred(key_list[14], (ROWS, LEN, D), 1.0, 6.0, ((0, 4), (1, 8)))
    return dict(layer_input=layer_input, doc_starts=doc_starts, norm1_gain=norm1_gain, w_query=w_query, w_forget=w_forget, w_input=w_input, w_gate_out=w_gate_out, forget_floor=forget_floor, group_gain=group_gain, w_out=w_out, norm2_gain=norm2_gain, ffn_gate=ffn_gate, ffn_up=ffn_up, ffn_down=ffn_down, out_cotangent=out_cotangent)


highest = lax.Precision.HIGHEST
epsilon = 1e-06

@jax.custom_vjp
def low(v):
    return lax.optimization_barrier(v.astype(jnp.bfloat16)).astype(jnp.float32)

@jax.custom_vjp
def low_back(v):
    return v

def low_keep(v):
    return (low(v), None)

def low_pass(kept, grad):
    return (grad,)

def back_keep(v):
    return (v, None)

def back_low(kept, grad):
    return (low(grad),)
low.defvjp(low_keep, low_pass)
low_back.defvjp(back_keep, back_low)

def rms_scale(tensor):
    return lax.rsqrt(lax.optimization_barrier(jnp.mean(tensor * tensor, axis=-1, keepdims=True)) + epsilon)

def mix_span(carry_state, span_items):

    def single_step(state_now, item):
        q_now, keep_now, add_now, value_now = item
        state_now = state_now * keep_now[:, :, None] + add_now[:, :, None] * value_now[:, None, :]
        return (state_now, jnp.einsum('hc,hcd->hd', q_now, state_now, precision=highest))
    return lax.scan(single_step, carry_state, span_items)

def row_forward(x_row, start_row, params):
    norm1_gain, w_query, w_forget, w_input, w_gate_out, forget_floor, group_gain, w_out, norm2_gain, ffn_gate, ffn_up, ffn_down = params
    normed = low(x_row * rms_scale(x_row) * norm1_gain)
    queries = low_back(jnp.dot(normed, w_query, precision=highest))
    forget_pre = low_back(jnp.dot(normed, w_forget, precision=highest))
    values = low_back(jnp.dot(normed, w_input, precision=highest))
    gate_pre = low_back(jnp.dot(normed, w_gate_out, precision=highest))
    inject = (1.0 - forget_floor) * jax.nn.sigmoid(-forget_pre)
    keeping = (1.0 - inject) * (1.0 - start_row.astype(jnp.float32))[:, None]
    span_len = 64 if LEN % 64 == 0 else LEN
    span_count = LEN // span_len

    def spans(tensor):
        return tensor.reshape(span_count, span_len, HEADS, HEAD_DIM)
    start_state = jnp.zeros((HEADS, HEAD_DIM, HEAD_DIM), jnp.float32)
    final_state, mixed = lax.scan(jax.checkpoint(mix_span), start_state, (spans(queries), spans(keeping), spans(inject), spans(values)))
    mixed = mixed.reshape(LEN, HEADS, HEAD_DIM)
    grouped = mixed * rms_scale(mixed) * group_gain.reshape(HEADS, HEAD_DIM)
    gated = low(grouped.reshape(LEN, D) * jax.nn.silu(gate_pre))
    mixer = low_back(jnp.dot(gated, w_out, precision=highest))
    resid = x_row + mixer
    ffn_in = low(resid * rms_scale(resid) * norm2_gain)
    gate_ff = low_back(jnp.dot(ffn_in, ffn_gate, precision=highest))
    up_ff = low_back(jnp.dot(ffn_in, ffn_up, precision=highest))
    inner_act = low(jax.nn.silu(gate_ff) * up_ff)
    return resid + jnp.dot(inner_act, ffn_down.T, precision=highest)

def reference(layer_input, doc_starts, norm1_gain, w_query, w_forget, w_input, w_gate_out, forget_floor, group_gain, w_out, norm2_gain, ffn_gate, ffn_up, ffn_down, out_cotangent):
    params = tuple((p.astype(jnp.float32) for p in (norm1_gain, w_query, w_forget, w_input, w_gate_out, forget_floor, group_gain, w_out, norm2_gain, ffn_gate, ffn_up, ffn_down)))
    inputs = layer_input.astype(jnp.float32)
    row_fn = jax.checkpoint(row_forward)

    def forward(inputs_now, params_now):

        def over_rows(carry, item):
            return (carry, row_fn(item[0], item[1], params_now))
        return lax.scan(over_rows, jnp.zeros((), jnp.float32), (inputs_now, doc_starts))[1]
    outputs, pullback = jax.vjp(forward, inputs, params)
    input_grad, grads = pullback(out_cotangent.astype(jnp.float32))
    return (outputs.astype(jnp.bfloat16), input_grad, grads[1], grads[2], grads[3], grads[4], grads[7], grads[6], grads[5], grads[0], grads[8], grads[9], grads[10], grads[11])
```

```python
import functools

import jax
import jax.numpy as jnp
from jax import lax
from jax.experimental import pallas as pl
from jax.experimental.pallas import tpu as pltpu
from jax.sharding import PartitionSpec as P

HEAD_DIM = 128
epsilon = 1e-06
f32 = jnp.float32
bf16 = jnp.bfloat16


def swap(tensor, bit, size):
    return lax.ppermute(tensor, "head", [(at, at ^ bit) for at in range(size)])


def mm(left, right, dims, out=f32):
    return lax.dot_general(left, right, (dims, ((), ())), preferred_element_type=out)


NN = ((1,), (0,))
NT = ((1,), (1,))
TN = ((0,), (0,))


def rms_scale(tensor):
    return lax.rsqrt(jnp.mean(tensor * tensor, axis=-1, keepdims=True) + epsilon)


def gather_near(own, bits, size):
    return swap(own, bits[0], size), swap(own, bits[1], size)


def gather_far(near, bits, size):
    half = near[0].shape[0] // 2
    return swap(near[0][:half], bits[1], size), swap(near[1][half:], bits[0], size)


def gather_chips(own, bits, size):
    if len(bits) == 2:
        near = gather_near(own, bits, size)
        return [own, *near, *gather_far(near, bits, size)]
    parts = [own]
    for bit in bits:
        moved = swap(jnp.stack(parts), bit, size)
        parts = parts + [moved[at] for at in range(len(parts))]
    return parts


def scatter_chips(part_of, bits, size):
    if len(bits) == 2:
        first, second = bits
        both = part_of(3).astype(bf16)
        half = both.shape[0] // 2
        top_both, bottom_both = swap(both[:half], first, size), swap(both[half:], second, size)
        at_first, at_second = part_of(1), part_of(2)
        top_first = swap(at_first[:half].astype(bf16), first, size)
        bottom_second = swap(at_second[half:].astype(bf16), second, size)
        bottom_first = swap(
            (at_first[half:].astype(f32) + bottom_both.astype(f32)).astype(bf16), first, size
        )
        top_second = swap(
            (at_second[:half].astype(f32) + top_both.astype(f32)).astype(bf16), second, size
        )
        own = part_of(0).astype(f32)
        top = own[:half] + top_first.astype(f32) + top_second.astype(f32)
        bottom = own[half:] + bottom_first.astype(f32) + bottom_second.astype(f32)
        return jnp.concatenate((top, bottom))
    parts = [part_of(at).astype(f32) for at in range(1 << len(bits))]
    for bit in reversed(bits):
        count = len(parts) // 2
        moved = swap(jnp.stack(parts[count:]).astype(bf16), bit, size)
        parts = [parts[at] + moved[at].astype(f32) for at in range(count)]
    return parts[0]


def after(tensor, *others):
    return lax.optimization_barrier((tensor,) + others)[0]


def halves(tensor):
    high = tensor.astype(bf16)
    return high, (tensor - high.astype(f32)).astype(bf16)


def cumulate(triangle, tensor):
    high, low = halves(tensor)
    return mm(triangle, high, NN) + mm(triangle, low, NN)


def span_masks(info, block, blocks, seg_ref):
    span = seg_ref.shape[-1]
    across = jnp.broadcast_to(seg_ref[0], (span, span))
    down = across.T
    rows = lax.broadcasted_iota(jnp.int32, (span, span), 0)
    cols = lax.broadcasted_iota(jnp.int32, (span, span), 1)
    before = info[1 + block]
    last = info[1 + blocks + block]
    same = (across == down) & (rows >= cols)
    column = down[:, :1]
    carried = (column == before).astype(f32)
    to_final = (column == last).astype(f32)
    through = (before == last).astype(f32)
    return rows, cols, same, carried, to_final, through


def head_columns(head, half_heads, half_width):
    base = (head // half_heads) * 4 * half_width + (head % half_heads) * HEAD_DIM
    return [slice(base + at * half_width, base + at * half_width + HEAD_DIM) for at in range(4)]


def forward_kernel(
    blocks, half_heads, info, proj_ref, floor_ref, gain_ref, seg_ref, gated_ref, mixed_ref, states_ref, scores_ref, state
):
    block = pl.program_id(0)
    half_width = half_heads * HEAD_DIM

    @pl.when(block == 0)
    def _():
        state[...] = jnp.zeros_like(state)

    rows, cols, same, carried, to_final, through = span_masks(info, block, blocks, seg_ref)
    span = rows.shape[0]
    lower = (rows >= cols).astype(bf16)
    for head in range(2 * half_heads):
        lanes = slice(head * HEAD_DIM, (head + 1) * HEAD_DIM)
        at_q, at_f, at_v, at_g = head_columns(head, half_heads, half_width)
        queries, forget_pre = proj_ref[:, at_q], proj_ref[:, at_f]
        values, gate = proj_ref[:, at_v].astype(bf16), proj_ref[:, at_g]
        inject = (1.0 - floor_ref[:, lanes]) / (1.0 + jnp.exp(forget_pre))
        decays = cumulate(lower, jnp.log(1.0 - inject))
        last = decays[span - 1 :, :]
        lifted, lifted_rest = halves(queries * jnp.exp(decays))
        lowered, lowered_rest = halves(inject * jnp.exp(-decays))
        scores = mm(lifted, lowered, NT) + mm(lifted, lowered_rest, NT) + mm(lifted_rest, lowered, NT)
        scores = jnp.where(same, scores, 0.0).astype(bf16)
        scores_ref[0, head] = scores
        now = state[head]
        states_ref[0, head] = now
        mixed = mm(scores, values, NN) + carried * mm(lifted, now.astype(bf16), NT)
        kept = (inject * jnp.exp(last - decays) * to_final).astype(bf16)
        state[head] = now * (jnp.exp(last) * through) + mm(values, kept, TN)
        mixed_ref[:, lanes] = mixed
        grouped = mixed * rms_scale(mixed) * gain_ref[:, lanes]
        gated_ref[:, lanes] = (grouped * gate / (1.0 + jnp.exp(-gate))).astype(bf16)


def backward_kernel(
    blocks, half_heads, info, proj_ref, floor_ref, gain_ref, seg_ref, mixed_ref, grad_ref, states_ref, scores_ref,
    proj_grad_ref, floor_grad_ref, gain_grad_ref, state_grad,
):
    step = pl.program_id(0)
    block = blocks - 1 - step
    half_width = half_heads * HEAD_DIM

    @pl.when(step == 0)
    def _():
        state_grad[...] = jnp.zeros_like(state_grad)
        floor_grad_ref[...] = jnp.zeros_like(floor_grad_ref)
        gain_grad_ref[...] = jnp.zeros_like(gain_grad_ref)

    rows, cols, same, carried, to_final, through = span_masks(info, block, blocks, seg_ref)
    span = rows.shape[0]
    lower = (rows >= cols).astype(bf16)
    upper = (rows <= cols).astype(bf16)
    is_last = lax.broadcasted_iota(jnp.int32, (span, 1), 0) == span - 1
    for head in range(2 * half_heads):
        lanes = slice(head * HEAD_DIM, (head + 1) * HEAD_DIM)
        at_q, at_f, at_v, at_g = head_columns(head, half_heads, half_width)
        queries, forget_pre = proj_ref[:, at_q], proj_ref[:, at_f]
        values, gate = proj_ref[:, at_v].astype(bf16), proj_ref[:, at_g]
        mixed, gain, grad = mixed_ref[:, lanes], gain_ref[:, lanes], grad_ref[:, lanes]
        gate_sig = 1.0 / (1.0 + jnp.exp(-gate))
        scale = rms_scale(mixed)
        unit = mixed * scale
        grouped_grad = grad * gate * gate_sig
        proj_grad_ref[:, at_g] = (
            grad * unit * gain * gate_sig * (1.0 + gate * (1.0 - gate_sig))
        ).astype(bf16)
        gain_grad_ref[:, lanes] += jnp.sum(grouped_grad * unit, axis=0, keepdims=True)
        unit_grad = grouped_grad * gain
        mixed_grad, mixed_rest = halves(
            scale * (unit_grad - unit * jnp.mean(unit_grad * unit, axis=-1, keepdims=True))
        )
        room = 1.0 - floor_ref[:, lanes]
        sig = 1.0 / (1.0 + jnp.exp(forget_pre))
        inject = room * sig
        decays = cumulate(lower, jnp.log(1.0 - inject))
        last = decays[span - 1 :, :]
        rise, fall, rest = jnp.exp(decays), jnp.exp(-decays), jnp.exp(last - decays) * to_final
        lifted = (queries * rise).astype(bf16)
        lowered = (inject * fall).astype(bf16)
        kept = (inject * rest).astype(bf16)
        scores = scores_ref[0, head]
        scores_grad = mm(mixed_grad, values, NT) + mm(mixed_rest, values, NT)
        scores_grad = jnp.where(same, scores_grad, 0.0).astype(bf16)
        now, after = states_ref[0, head], state_grad[head]
        after_low, now_low = after.astype(bf16), now.astype(bf16)
        state_part = mm(mixed_grad, now_low, NN) + mm(mixed_rest, now_low, NN)
        lifted_grad = mm(scores_grad, lowered, NN) + carried * state_part
        lowered_grad = mm(scores_grad, lifted, TN)
        kept_grad = mm(values, after_low, NN)
        value_grad = mm(scores, mixed_grad, TN) + mm(kept, after_low, NT)
        kept_term = kept_grad * kept.astype(f32)
        decay_grad = lifted_grad * lifted.astype(f32) - lowered_grad * lowered.astype(f32) - kept_term
        pass_on = jnp.exp(last) * through
        last_grad = jnp.sum(kept_term, axis=0, keepdims=True) + pass_on * jnp.sum(
            now * after, axis=0, keepdims=True
        )
        decay_grad = decay_grad + jnp.where(is_last, last_grad, 0.0)
        log_grad = cumulate(upper, decay_grad)
        inject_grad = lowered_grad * fall + kept_grad * rest - log_grad / (1.0 - inject)
        state_grad[head] = after * pass_on + mm(
            mixed_grad, (lifted.astype(f32) * carried).astype(bf16), TN
        )
        proj_grad_ref[:, at_q] = (lifted_grad * rise).astype(bf16)
        proj_grad_ref[:, at_f] = (-inject_grad * room * sig * (1.0 - sig)).astype(bf16)
        proj_grad_ref[:, at_v] = value_grad.astype(bf16)
        floor_grad_ref[:, lanes] -= jnp.sum(inject_grad * sig, axis=0, keepdims=True)


def recurrence(info, proj, floor_row, gain_row, seg, half_heads, size):
    blocks, _, span = seg.shape
    width = floor_row.shape[1]
    spot = lambda block, info: (block ^ info[0], 0)
    fixed = lambda block, info: (0, 0)
    return pl.pallas_call(
        functools.partial(forward_kernel, blocks, half_heads),
        out_shape=(
            jax.ShapeDtypeStruct((blocks * span, width), bf16),
            jax.ShapeDtypeStruct((blocks * span, width), f32),
            jax.ShapeDtypeStruct((blocks, 2 * half_heads, HEAD_DIM, HEAD_DIM), f32),
            jax.ShapeDtypeStruct((blocks, 2 * half_heads, span, span), bf16),
        ),
        grid_spec=pltpu.PrefetchScalarGridSpec(
            num_scalar_prefetch=1,
            grid=(blocks,),
            in_specs=[
                pl.BlockSpec((span, 4 * width), spot),
                pl.BlockSpec((1, width), fixed),
                pl.BlockSpec((1, width), fixed),
                pl.BlockSpec((1, 1, span), lambda block, info: (block, 0, 0)),
            ],
            out_specs=[
                pl.BlockSpec((span, width), spot),
                pl.BlockSpec((span, width), spot),
                pl.BlockSpec(
                    (1, 2 * half_heads, HEAD_DIM, HEAD_DIM), lambda block, info: (block, 0, 0, 0)
                ),
                pl.BlockSpec((1, 2 * half_heads, span, span), lambda block, info: (block, 0, 0, 0)),
            ],
            scratch_shapes=[pltpu.VMEM((2 * half_heads, HEAD_DIM, HEAD_DIM), f32)],
        ),
        compiler_params=pltpu.CompilerParams(vmem_limit_bytes=24 * 1024 * 1024),
        cost_estimate=pl.CostEstimate(
            flops=blocks * 2 * half_heads * 16 * HEAD_DIM**3, bytes_accessed=16 * 2**20, transcendentals=0
        ),
    )(info, proj, floor_row, gain_row, seg)


def recurrence_back(info, proj, floor_row, gain_row, seg, mixed, grad, states, scores, half_heads, size):
    blocks, _, span = seg.shape
    width = floor_row.shape[1]
    spot = lambda step, info: ((blocks - 1 - step) ^ info[0], 0)
    fixed = lambda step, info: (0, 0)
    return pl.pallas_call(
        functools.partial(backward_kernel, blocks, half_heads),
        out_shape=(
            jax.ShapeDtypeStruct((blocks * span, 4 * width), bf16),
            jax.ShapeDtypeStruct((1, width), f32),
            jax.ShapeDtypeStruct((1, width), f32),
        ),
        grid_spec=pltpu.PrefetchScalarGridSpec(
            num_scalar_prefetch=1,
            grid=(blocks,),
            in_specs=[
                pl.BlockSpec((span, 4 * width), spot),
                pl.BlockSpec((1, width), fixed),
                pl.BlockSpec((1, width), fixed),
                pl.BlockSpec((1, 1, span), lambda step, info: (blocks - 1 - step, 0, 0)),
                pl.BlockSpec((span, width), spot),
                pl.BlockSpec((span, width), spot),
                pl.BlockSpec(
                    (1, 2 * half_heads, HEAD_DIM, HEAD_DIM),
                    lambda step, info: (blocks - 1 - step, 0, 0, 0),
                ),
                pl.BlockSpec(
                    (1, 2 * half_heads, span, span), lambda step, info: (blocks - 1 - step, 0, 0, 0)
                ),
            ],
            out_specs=[
                pl.BlockSpec((span, 4 * width), spot),
                pl.BlockSpec((1, width), fixed),
                pl.BlockSpec((1, width), fixed),
            ],
            scratch_shapes=[pltpu.VMEM((2 * half_heads, HEAD_DIM, HEAD_DIM), f32)],
        ),
        compiler_params=pltpu.CompilerParams(vmem_limit_bytes=24 * 1024 * 1024),
        cost_estimate=pl.CostEstimate(
            flops=blocks * 2 * half_heads * 32 * HEAD_DIM**3, bytes_accessed=24 * 2**20, transcendentals=0
        ),
    )(info, proj, floor_row, gain_row, seg, mixed, grad, states, scores)


def per_device(
    size,
    depth,
    layer_input,
    doc_starts,
    norm1_gain,
    w_query,
    w_forget,
    w_input,
    w_gate_out,
    forget_floor,
    group_gain,
    w_out,
    norm2_gain,
    ffn_gate,
    ffn_up,
    ffn_down,
    out_cotangent,
):
    row_count, shard_len, model_width = layer_input.shape
    assert row_count == 2 and size & (size - 1) == 0
    seq_len = doc_starts.shape[1]
    half_width = w_query.shape[1]
    half_heads = half_width // HEAD_DIM
    width = 2 * half_width
    me = lax.axis_index("head")
    place = lax.axis_index("dp")
    row = me % 2
    bits = [1 << at for at in range(1, size.bit_length() - 1)]
    own_tokens = 2 * shard_len
    hidden_dev = ffn_gate.shape[1]
    hidden_half = depth * hidden_dev

    def pick(tensor, at):
        return lax.dynamic_index_in_dim(tensor, at, 0, keepdims=False)

    def to_row(tensor):
        return jnp.concatenate((pick(tensor, row), swap(pick(tensor, 1 - row), 1, size)))

    def from_row(tensor):
        mine, other = tensor[:shard_len], swap(tensor[shard_len:], 1, size)
        return jnp.where(row == 0, jnp.stack((mine, other)), jnp.stack((other, mine)))

    def chunk(tensor, at):
        return tensor[at * own_tokens : (at + 1) * own_tokens]

    gate_up = lax.all_gather(jnp.stack((ffn_gate.T, ffn_up.T)), "dp", axis=1, tiled=True)
    down = lax.all_gather(after(ffn_down.T, gate_up), "dp", axis=0, tiled=True)

    own_rows = to_row(layer_input).astype(f32)
    input_scale = rms_scale(own_rows)
    normed_own = (own_rows * input_scale * norm1_gain).astype(bf16)
    normed_parts = gather_chips(normed_own, bits, size)
    normed = jnp.concatenate(normed_parts)

    proj_own = jnp.concatenate((w_query, w_forget, w_input, w_gate_out), axis=1)
    proj_weights = jnp.concatenate((proj_own, swap(proj_own, 1, size)), axis=1)
    out_weights = jnp.concatenate((w_out, swap(w_out, 1, size)))
    vectors = jnp.stack((forget_floor, group_gain))
    vectors = jnp.concatenate((vectors, swap(vectors, 1, size)), axis=1)
    floor_row, gain_row = vectors[:1], vectors[1:]

    seg = jnp.cumsum(pick(doc_starts, row)).reshape(size, shard_len)
    seg_last = seg[:, -1]
    info = jnp.concatenate((me[None], jnp.zeros((1,), jnp.int32), seg_last[:-1], seg_last))
    seg = seg[:, None, :]

    proj = mm(normed, proj_weights, NN)
    gated, mixed, states, scores = recurrence(info, proj, floor_row, gain_row, seg, half_heads, size)
    cot_own = to_row(out_cotangent)
    if len(bits) == 2:
        cot_near = gather_near(after(cot_own, *normed_parts), bits, size)

    resid = own_rows + scatter_chips(
        lambda at: mm(chunk(gated, at), out_weights, NN).astype(bf16), bits, size
    )
    row_scale = rms_scale(resid)
    ffn_own = (resid * row_scale * norm2_gain).astype(bf16)
    ffn_parts = gather_chips(ffn_own, bits, size)
    ffn_in = jnp.concatenate(ffn_parts)
    if len(bits) == 2:
        cot_held = [after(near, *ffn_parts) for near in cot_near]
        cot_parts = [cot_own, *cot_near, *gather_far(cot_held, bits, size)]
    else:
        cot_parts = gather_chips(after(cot_own, *ffn_parts), bits, size)
    cot = jnp.concatenate(cot_parts)

    gate_up = jnp.concatenate((gate_up, swap(gate_up, 1, size)), axis=1)
    gate_rows, up_rows = gate_up[0], gate_up[1]
    down_rows = jnp.concatenate((down, swap(down, 1, size)))
    gate_ff = mm(ffn_in, gate_rows, NT)
    up_ff = mm(ffn_in, up_rows, NT)
    gate_sig = jax.nn.sigmoid(gate_ff)
    inner = (gate_ff * gate_sig * up_ff).astype(bf16)

    def pair_grad(left, right, cut):
        other = swap(mm(left[:, cut:], right, TN).astype(bf16), 1, size)
        return (mm(left[:, :cut], right, TN) + other.astype(f32)).astype(bf16)

    down_grad = pair_grad(inner, cot, hidden_half)
    ffn_down_grad = lax.psum_scatter(down_grad, "dp", scatter_dimension=0, tiled=True)

    inner_grad = mm(cot, down_rows, NT)
    gate_grad = (inner_grad * up_ff * gate_sig * (1.0 + gate_ff * (1.0 - gate_sig))).astype(bf16)
    up_grad = (inner_grad * gate_ff * gate_sig).astype(bf16)
    ffn_in_grad = scatter_chips(
        lambda at: (
            mm(chunk(gate_grad, at), gate_rows, NN) + mm(chunk(up_grad, at), up_rows, NN)
        ).astype(bf16),
        bits,
        size,
    )
    gate_up_grad = jnp.stack(
        (pair_grad(gate_grad, ffn_in, hidden_half), pair_grad(up_grad, ffn_in, hidden_half))
    )
    gate_up_grad = lax.psum_scatter(
        after(gate_up_grad, down_grad), "dp", scatter_dimension=1, tiled=True
    )

    scaled = ffn_in_grad * norm2_gain
    resid_grad = cot_own.astype(f32) + row_scale * (
        scaled - resid * row_scale * row_scale * jnp.mean(scaled * resid, axis=-1, keepdims=True)
    )
    norm2_part = jnp.sum(ffn_in_grad * resid * row_scale, axis=0)
    mixer_parts = gather_chips(resid_grad.astype(bf16), bits, size)
    mixer_grad = jnp.concatenate(mixer_parts)

    inner_late = after(inner, *mixer_parts)
    output = resid + scatter_chips(
        lambda at: mm(chunk(inner_late, at), down_rows, NN).astype(bf16), bits, size
    )
    output = from_row(output.astype(bf16))

    gated_grad = mm(mixer_grad, out_weights, NT)
    proj_grad, floor_grad, gain_grad = recurrence_back(
        info, proj, floor_row, gain_row, seg, mixed, gated_grad, states, scores, half_heads, size
    )
    normed_grad = scatter_chips(
        lambda at: mm(chunk(proj_grad, at), proj_weights, NT).astype(bf16), bits, size
    )
    scaled_in = normed_grad * norm1_gain
    input_grad = resid_grad + input_scale * (
        scaled_in
        - own_rows
        * input_scale
        * input_scale
        * jnp.mean(scaled_in * own_rows, axis=-1, keepdims=True)
    )
    norm1_part = jnp.sum(normed_grad * own_rows * input_scale, axis=0)
    input_grad = from_row(input_grad)

    out_grad = pair_grad(gated, mixer_grad, half_width)
    proj_w_grad = mm(normed, proj_grad[:, 2 * width :], TN).astype(bf16)
    proj_w_grad = mm(normed, proj_grad[:, : 2 * width], TN) + swap(proj_w_grad, 1, size).astype(f32)
    proj_w_grad = lax.psum_scatter(
        proj_w_grad.astype(bf16), "dp", scatter_dimension=0, tiled=True
    ).astype(f32)
    out_grad = lax.psum_scatter(out_grad, "dp", scatter_dimension=1, tiled=True)

    vector_grads = jnp.concatenate((gain_grad, floor_grad))
    vector_grads = vector_grads[:, :half_width] + swap(vector_grads[:, half_width:], 1, size)
    moved = [
        lax.ppermute(vector_grads, "dp", [(at, (at + slot) % depth) for at in range(depth)])
        for slot in range(1, depth)
    ]
    vector_grads = sum(moved, vector_grads)
    vector_len = half_width // depth
    vector_grads = lax.dynamic_slice_in_dim(vector_grads, place * vector_len, vector_len, 1)
    norm_grads = jnp.stack((norm1_part, norm2_part))
    for bit in [1] + bits:
        norm_grads = norm_grads + swap(norm_grads, bit, size)
    moved = [
        lax.ppermute(norm_grads, "dp", [(at, (at + slot) % depth) for at in range(depth)])
        for slot in range(1, depth)
    ]
    stacked = jnp.stack([norm_grads] + moved)
    order = (place - jnp.arange(depth)) % depth
    norm_grads = jnp.sum(jnp.zeros_like(stacked).at[order].set(stacked), axis=0)

    return (
        output,
        input_grad,
        proj_w_grad[:, 0:half_width],
        proj_w_grad[:, half_width : 2 * half_width],
        proj_w_grad[:, 2 * half_width : 3 * half_width],
        proj_w_grad[:, 3 * half_width : 4 * half_width],
        out_grad.astype(f32),
        vector_grads[0],
        vector_grads[1],
        norm_grads[0],
        norm_grads[1],
        gate_up_grad[0].astype(f32).T,
        gate_up_grad[1].astype(f32).T,
        ffn_down_grad.astype(f32).T,
    )


def solution(mesh):
    placed = (
        P("dp", "head", None),
        P("dp", None),
        P(),
        P(None, "head"),
        P(None, "head"),
        P(None, "head"),
        P(None, "head"),
        P("head"),
        P("head"),
        P("head", None),
        P(),
        P(None, ("head", "dp")),
        P(None, ("head", "dp")),
        P(None, ("head", "dp")),
        P("dp", "head", None),
    )
    return jax.shard_map(
        functools.partial(per_device, mesh.shape["head"], mesh.shape["dp"]),
        mesh=mesh,
        in_specs=placed,
        out_specs=(
            P("dp", "head", None),
            P("dp", "head", None),
            P("dp", "head"),
            P("dp", "head"),
            P("dp", "head"),
            P("dp", "head"),
            P("head", "dp"),
            P(("head", "dp")),
            P(("head", "dp")),
            P(),
            P(),
            P(None, ("head", "dp")),
            P(None, ("head", "dp")),
            P(None, ("head", "dp")),
        ),
        check_vma=False,
    )
```

```python
import functools

import jax
import jax.numpy as jnp
from jax import lax
from jax.experimental import pallas as pl
from jax.experimental.pallas import tpu as pltpu
from jax.sharding import PartitionSpec as P

HEAD_DIM = 128
epsilon = 1e-06
f32 = jnp.float32
bf16 = jnp.bfloat16


def swap(tensor, bit, size):
    return lax.ppermute(tensor, "head", [(at, at ^ bit) for at in range(size)])


def mm(left, right, dims, out=f32):
    return lax.dot_general(left, right, (dims, ((), ())), preferred_element_type=out)


NN = ((1,), (0,))
NT = ((1,), (1,))
TN = ((0,), (0,))


def rms_scale(tensor):
    return lax.rsqrt(jnp.mean(tensor * tensor, axis=-1, keepdims=True) + epsilon)


def gather_near(own, bits, size):
    return swap(own, bits[0], size), swap(own, bits[1], size)


def gather_far(near, bits, size):
    half = near[0].shape[0] // 2
    return swap(near[0][:half], bits[1], size), swap(near[1][half:], bits[0], size)


def gather_start(own, bits, size):
    if len(bits) == 2:
        near = gather_near(own, bits, size)
        return near, [own, *near, *gather_far(near, bits, size)]
    parts = [own]
    for bit in bits:
        moved = swap(jnp.stack(parts), bit, size)
        parts = parts + [moved[at] for at in range(len(parts))]
    return parts[1:], parts


class Scatter:
    def __init__(self, part_of, bits, size):
        self.bits, self.size = bits, size
        self.moved, self.sends = [], None
        if len(bits) == 2:
            first, second = bits
            both = part_of(3)
            self.half = half = both.shape[0] // 2
            top_both, bottom_both = swap(both[:half], first, size), swap(both[half:], second, size)
            self.at_first, self.at_second = part_of(1), part_of(2)
            top_first = swap(self.at_first[:half], first, size)
            bottom_second = swap(self.at_second[half:], second, size)
            self.moved = [top_both, bottom_both, top_first, bottom_second]
            self.own = part_of(0)
        else:
            self.parts = [part_of(at) for at in range(1 << len(bits))]

    def finish(self):
        self.moved = list(tie(*self.moved))
        top_both, bottom_both = self.moved[:2]
        self.sends = (
            add(self.at_first[self.half :], bottom_both).astype(bf16),
            add(self.at_second[: self.half], top_both).astype(bf16),
        )

    def total(self, held=None):
        bits, size = self.bits, self.size
        if len(bits) == 2:
            first, second = bits
            if self.sends is None:
                self.finish()
            bottom_first, top_second = swap(self.sends[0], first, size), swap(self.sends[1], second, size)
            bottom_first, top_second, held = tie(bottom_first, top_second, held)
            top_first, bottom_second = self.moved[2:]
            top = add(self.own[: self.half], top_first, top_second)
            bottom = add(self.own[self.half :], bottom_first, bottom_second)
            return jnp.concatenate((top, bottom)), held
        parts = [part.astype(f32) for part in self.parts]
        for bit in reversed(bits):
            count = len(parts) // 2
            moved = swap(jnp.stack(parts[count:]).astype(bf16), bit, size)
            parts = [add(parts[at], moved[at]) for at in range(count)]
        return parts[0], held


def add(first, *rest):
    total = first.astype(f32)
    for term in rest:
        total = total + term.astype(f32)
    return total


def tie(*tensors):
    return lax.optimization_barrier(tensors)


def halves(tensor):
    high = tensor.astype(bf16)
    return high, (tensor - high.astype(f32)).astype(bf16)


def cumulate(triangle, tensor):
    high, low = halves(tensor)
    return mm(triangle, high, NN) + mm(triangle, low, NN)


def span_masks(info, block, blocks, seg_ref):
    span = seg_ref.shape[-1]
    across = jnp.broadcast_to(seg_ref[0], (span, span))
    down = across.T
    rows = lax.broadcasted_iota(jnp.int32, (span, span), 0)
    cols = lax.broadcasted_iota(jnp.int32, (span, span), 1)
    before = info[1 + block]
    last = info[1 + blocks + block]
    same = (across == down) & (rows >= cols)
    column = down[:, :1]
    carried = (column == before).astype(f32)
    to_final = (column == last).astype(f32)
    through = (before == last).astype(f32)
    return rows, cols, same, carried, to_final, through


def head_columns(head, half_heads, half_width):
    base = (head // half_heads) * 4 * half_width + (head % half_heads) * HEAD_DIM
    return [slice(base + at * half_width, base + at * half_width + HEAD_DIM) for at in range(4)]


def forward_kernel(
    blocks, half_heads, info, proj_ref, floor_ref, gain_ref, seg_ref, gated_ref, mixed_ref, states_ref, scores_ref, state
):
    block = pl.program_id(0)
    half_width = half_heads * HEAD_DIM

    @pl.when(block == 0)
    def _():
        state[...] = jnp.zeros_like(state)

    rows, cols, same, carried, to_final, through = span_masks(info, block, blocks, seg_ref)
    span = rows.shape[0]
    lower = (rows >= cols).astype(bf16)
    for head in range(2 * half_heads):
        lanes = slice(head * HEAD_DIM, (head + 1) * HEAD_DIM)
        at_q, at_f, at_v, at_g = head_columns(head, half_heads, half_width)
        queries, forget_pre = proj_ref[:, at_q], proj_ref[:, at_f]
        values, gate = proj_ref[:, at_v].astype(bf16), proj_ref[:, at_g]
        inject = (1.0 - floor_ref[:, lanes]) / (1.0 + jnp.exp(forget_pre))
        decays = cumulate(lower, jnp.log(1.0 - inject))
        last = decays[span - 1 :, :]
        lifted, lifted_rest = halves(queries * jnp.exp(decays))
        lowered, lowered_rest = halves(inject * jnp.exp(-decays))
        scores = mm(lifted, lowered, NT) + mm(lifted, lowered_rest, NT) + mm(lifted_rest, lowered, NT)
        scores = jnp.where(same, scores, 0.0).astype(bf16)
        scores_ref[0, head] = scores
        now = state[head]
        states_ref[0, head] = now
        mixed = mm(scores, values, NN) + carried * mm(lifted, now.astype(bf16), NT)
        kept = (inject * jnp.exp(last - decays) * to_final).astype(bf16)
        state[head] = now * (jnp.exp(last) * through) + mm(values, kept, TN)
        mixed_ref[:, lanes] = mixed
        grouped = mixed * rms_scale(mixed) * gain_ref[:, lanes]
        gated_ref[:, lanes] = (grouped * gate / (1.0 + jnp.exp(-gate))).astype(bf16)


def backward_kernel(
    blocks, half_heads, info, proj_ref, floor_ref, gain_ref, seg_ref, mixed_ref, grad_ref, states_ref, scores_ref,
    proj_grad_ref, floor_grad_ref, gain_grad_ref, state_grad,
):
    step = pl.program_id(0)
    block = blocks - 1 - step
    half_width = half_heads * HEAD_DIM

    @pl.when(step == 0)
    def _():
        state_grad[...] = jnp.zeros_like(state_grad)
        floor_grad_ref[...] = jnp.zeros_like(floor_grad_ref)
        gain_grad_ref[...] = jnp.zeros_like(gain_grad_ref)

    rows, cols, same, carried, to_final, through = span_masks(info, block, blocks, seg_ref)
    span = rows.shape[0]
    lower = (rows >= cols).astype(bf16)
    upper = (rows <= cols).astype(bf16)
    is_last = lax.broadcasted_iota(jnp.int32, (span, 1), 0) == span - 1
    for head in range(2 * half_heads):
        lanes = slice(head * HEAD_DIM, (head + 1) * HEAD_DIM)
        at_q, at_f, at_v, at_g = head_columns(head, half_heads, half_width)
        queries, forget_pre = proj_ref[:, at_q], proj_ref[:, at_f]
        values, gate = proj_ref[:, at_v].astype(bf16), proj_ref[:, at_g]
        mixed, gain, grad = mixed_ref[:, lanes], gain_ref[:, lanes], grad_ref[:, lanes]
        gate_sig = 1.0 / (1.0 + jnp.exp(-gate))
        scale = rms_scale(mixed)
        unit = mixed * scale
        grouped_grad = grad * gate * gate_sig
        proj_grad_ref[:, at_g] = (
            grad * unit * gain * gate_sig * (1.0 + gate * (1.0 - gate_sig))
        ).astype(bf16)
        gain_grad_ref[:, lanes] += jnp.sum(grouped_grad * unit, axis=0, keepdims=True)
        unit_grad = grouped_grad * gain
        mixed_grad, mixed_rest = halves(
            scale * (unit_grad - unit * jnp.mean(unit_grad * unit, axis=-1, keepdims=True))
        )
        room = 1.0 - floor_ref[:, lanes]
        sig = 1.0 / (1.0 + jnp.exp(forget_pre))
        inject = room * sig
        decays = cumulate(lower, jnp.log(1.0 - inject))
        last = decays[span - 1 :, :]
        rise, fall, rest = jnp.exp(decays), jnp.exp(-decays), jnp.exp(last - decays) * to_final
        lifted = (queries * rise).astype(bf16)
        lowered = (inject * fall).astype(bf16)
        kept = (inject * rest).astype(bf16)
        scores = scores_ref[0, head]
        scores_grad = mm(mixed_grad, values, NT) + mm(mixed_rest, values, NT)
        scores_grad = jnp.where(same, scores_grad, 0.0).astype(bf16)
        now, after = states_ref[0, head], state_grad[head]
        after_low, now_low = after.astype(bf16), now.astype(bf16)
        state_part = mm(mixed_grad, now_low, NN) + mm(mixed_rest, now_low, NN)
        lifted_grad = mm(scores_grad, lowered, NN) + carried * state_part
        lowered_grad = mm(scores_grad, lifted, TN)
        kept_grad = mm(values, after_low, NN)
        value_grad = mm(scores, mixed_grad, TN) + mm(kept, after_low, NT)
        kept_term = kept_grad * kept.astype(f32)
        decay_grad = lifted_grad * lifted.astype(f32) - lowered_grad * lowered.astype(f32) - kept_term
        pass_on = jnp.exp(last) * through
        last_grad = jnp.sum(kept_term, axis=0, keepdims=True) + pass_on * jnp.sum(
            now * after, axis=0, keepdims=True
        )
        decay_grad = decay_grad + jnp.where(is_last, last_grad, 0.0)
        log_grad = cumulate(upper, decay_grad)
        inject_grad = lowered_grad * fall + kept_grad * rest - log_grad / (1.0 - inject)
        state_grad[head] = after * pass_on + mm(
            mixed_grad, (lifted.astype(f32) * carried).astype(bf16), TN
        )
        proj_grad_ref[:, at_q] = (lifted_grad * rise).astype(bf16)
        proj_grad_ref[:, at_f] = (-inject_grad * room * sig * (1.0 - sig)).astype(bf16)
        proj_grad_ref[:, at_v] = value_grad.astype(bf16)
        floor_grad_ref[:, lanes] -= jnp.sum(inject_grad * sig, axis=0, keepdims=True)


def recurrence(info, proj, floor_row, gain_row, seg, half_heads, size):
    blocks, _, span = seg.shape
    width = floor_row.shape[1]
    spot = lambda block, info: (block ^ info[0], 0)
    fixed = lambda block, info: (0, 0)
    return pl.pallas_call(
        functools.partial(forward_kernel, blocks, half_heads),
        out_shape=(
            jax.ShapeDtypeStruct((blocks * span, width), bf16),
            jax.ShapeDtypeStruct((blocks * span, width), f32),
            jax.ShapeDtypeStruct((blocks, 2 * half_heads, HEAD_DIM, HEAD_DIM), f32),
            jax.ShapeDtypeStruct((blocks, 2 * half_heads, span, span), bf16),
        ),
        grid_spec=pltpu.PrefetchScalarGridSpec(
            num_scalar_prefetch=1,
            grid=(blocks,),
            in_specs=[
                pl.BlockSpec((span, 4 * width), spot),
                pl.BlockSpec((1, width), fixed),
                pl.BlockSpec((1, width), fixed),
                pl.BlockSpec((1, 1, span), lambda block, info: (block, 0, 0)),
            ],
            out_specs=[
                pl.BlockSpec((span, width), spot),
                pl.BlockSpec((span, width), spot),
                pl.BlockSpec(
                    (1, 2 * half_heads, HEAD_DIM, HEAD_DIM), lambda block, info: (block, 0, 0, 0)
                ),
                pl.BlockSpec((1, 2 * half_heads, span, span), lambda block, info: (block, 0, 0, 0)),
            ],
            scratch_shapes=[pltpu.VMEM((2 * half_heads, HEAD_DIM, HEAD_DIM), f32)],
        ),
        compiler_params=pltpu.CompilerParams(vmem_limit_bytes=16 * 2**20),
        cost_estimate=pl.CostEstimate(
            flops=0, bytes_accessed=0, transcendentals=0
        ),
    )(info, proj, floor_row, gain_row, seg)


def recurrence_back(info, proj, floor_row, gain_row, seg, mixed, grad, states, scores, half_heads, size):
    blocks, _, span = seg.shape
    width = floor_row.shape[1]
    spot = lambda step, info: ((blocks - 1 - step) ^ info[0], 0)
    fixed = lambda step, info: (0, 0)
    return pl.pallas_call(
        functools.partial(backward_kernel, blocks, half_heads),
        out_shape=(
            jax.ShapeDtypeStruct((blocks * span, 4 * width), bf16),
            jax.ShapeDtypeStruct((1, width), f32),
            jax.ShapeDtypeStruct((1, width), f32),
        ),
        grid_spec=pltpu.PrefetchScalarGridSpec(
            num_scalar_prefetch=1,
            grid=(blocks,),
            in_specs=[
                pl.BlockSpec((span, 4 * width), spot),
                pl.BlockSpec((1, width), fixed),
                pl.BlockSpec((1, width), fixed),
                pl.BlockSpec((1, 1, span), lambda step, info: (blocks - 1 - step, 0, 0)),
                pl.BlockSpec((span, width), spot),
                pl.BlockSpec((span, width), spot),
                pl.BlockSpec(
                    (1, 2 * half_heads, HEAD_DIM, HEAD_DIM),
                    lambda step, info: (blocks - 1 - step, 0, 0, 0),
                ),
                pl.BlockSpec(
                    (1, 2 * half_heads, span, span), lambda step, info: (blocks - 1 - step, 0, 0, 0)
                ),
            ],
            out_specs=[
                pl.BlockSpec((span, 4 * width), spot),
                pl.BlockSpec((1, width), fixed),
                pl.BlockSpec((1, width), fixed),
            ],
            scratch_shapes=[pltpu.VMEM((2 * half_heads, HEAD_DIM, HEAD_DIM), f32)],
        ),
        compiler_params=pltpu.CompilerParams(vmem_limit_bytes=20 * 2**20),
        cost_estimate=pl.CostEstimate(
            flops=0, bytes_accessed=0, transcendentals=0
        ),
    )(info, proj, floor_row, gain_row, seg, mixed, grad, states, scores)


def stack_kernel(count, own, other, *refs):
    outs, sems = refs[:count], refs[count]
    half = own.shape[1]
    copies = []
    for at in range(count):
        for side, source in enumerate((own, other)):
            target = outs[at].at[pl.ds(side * half, half)]
            copies.append(pltpu.make_async_copy(source.at[at], target, sems.at[at, side]))
    for copy in copies:
        copy.start()
    for copy in copies:
        copy.wait()


def stack_rows(own, other):
    count, rows, depth = own.shape
    return pl.pallas_call(
        functools.partial(stack_kernel, count),
        out_shape=[jax.ShapeDtypeStruct((2 * rows, depth), own.dtype)] * count,
        in_specs=[pl.BlockSpec(memory_space=pl.ANY)] * 2,
        out_specs=[pl.BlockSpec(memory_space=pltpu.VMEM)] * count,
        scratch_shapes=[pltpu.SemaphoreType.DMA((count, 2))],
        compiler_params=pltpu.CompilerParams(vmem_limit_bytes=4 * 2**20),
        cost_estimate=pl.CostEstimate(flops=0, bytes_accessed=0, transcendentals=0),
    )(own, other)


def add_kernel(left, right, out):
    out[...] = (left[...].astype(f32) + right[...].astype(f32)).astype(bf16)


def add_pair(left, right):
    rows, depth = left.shape
    step = rows
    while step > 256 and step % 32 == 0:
        step //= 2
    block = pl.BlockSpec((step, depth), lambda at: (at, 0))
    return pl.pallas_call(
        add_kernel,
        out_shape=jax.ShapeDtypeStruct((rows, depth), bf16),
        grid=(rows // step,),
        in_specs=[block] * 2,
        out_specs=block,
        compiler_params=pltpu.CompilerParams(vmem_limit_bytes=10 * 2**20),
        cost_estimate=pl.CostEstimate(flops=0, bytes_accessed=0, transcendentals=0),
    )(left, right)


def cross_kernel(groups, count, left_cols, right_cols, *refs):
    lefts, rights = refs[: sum(groups)], refs[sum(groups) : sum(groups) + count]
    out, left_held, right_held, out_held, left_sem, right_sem, out_sem = refs[sum(groups) + count :]
    rows, width = out.shape[1:]
    spare = left_cols % 128
    step = out_held.shape[3]
    tiles = width // step
    left_copies, right_copies = [], [[] for _ in range(tiles)]
    at = 0
    for group, many in enumerate(groups):
        first = 0
        for ref in lefts[at : at + many]:
            here = pl.ds(first, ref.shape[0])
            left_copies.append(
                pltpu.make_async_copy(ref, left_held.at[group, here], left_sem.at[len(left_copies)])
            )
            first += ref.shape[0]
        at += many
    for tile in range(tiles):
        first = 0
        for index, ref in enumerate(rights):
            source = ref.at[:, pl.ds(right_cols + tile * step, step)]
            target = right_held.at[tile, pl.ds(first, ref.shape[0])]
            right_copies[tile].append(
                pltpu.make_async_copy(source, target, right_sem.at[tile, index])
            )
            first += ref.shape[0]
    for copy in right_copies[0] + left_copies:
        copy.start()
    for copies in right_copies[1:]:
        for copy in copies:
            copy.start()
    for copy in left_copies:
        copy.wait()
    out_copies = []
    for tile in range(tiles):
        for copy in right_copies[tile]:
            copy.wait()
        for group in range(len(groups)):
            left = left_held[group, :, left_cols - spare : left_cols + rows]
            product = mm(left, right_held[tile], TN)
            out_held[tile, group] = product[spare:].astype(bf16)
            out_copies.append(
                pltpu.make_async_copy(
                    out_held.at[tile, group],
                    out.at[group, :, pl.ds(tile * step, step)],
                    out_sem.at[tile, group],
                )
            )
            out_copies[-1].start()
    for copy in out_copies:
        copy.wait()


def cross(groups, rights, left_cols=None, right_cols=None):
    tokens = sum(part.shape[0] for part in rights)
    left_width, right_width = groups[0][0].shape[1], rights[0].shape[1]
    left_cols, right_cols = left_cols or (0, left_width), right_cols or (0, right_width)
    rows, width = left_cols[1], right_cols[1]
    step = 512 if width % 512 == 0 else width
    tiles, many = width // step, len(groups)
    anywhere = pl.BlockSpec(memory_space=pl.ANY)
    args = [part for group in groups for part in group] + list(rights)
    return pl.pallas_call(
        functools.partial(
            cross_kernel, [len(group) for group in groups], len(rights), left_cols[0], right_cols[0]
        ),
        out_shape=jax.ShapeDtypeStruct((many, rows, width), bf16),
        in_specs=[anywhere] * len(args),
        out_specs=anywhere,
        scratch_shapes=[
            pltpu.VMEM((many, tokens, left_width), bf16),
            pltpu.VMEM((tiles, tokens, step), bf16),
            pltpu.VMEM((tiles, many, rows, step), bf16),
            pltpu.SemaphoreType.DMA((len(args) - len(rights),)),
            pltpu.SemaphoreType.DMA((tiles, len(rights))),
            pltpu.SemaphoreType.DMA((tiles, many)),
        ],
        compiler_params=pltpu.CompilerParams(
            vmem_limit_bytes=2 * (many * tokens * left_width + tokens * width + many * rows * width)
            + 10 * 2**20
        ),
        cost_estimate=pl.CostEstimate(flops=0, bytes_accessed=0, transcendentals=0),
    )(*args)


def per_device(
    size,
    depth,
    layer_input,
    doc_starts,
    norm1_gain,
    w_query,
    w_forget,
    w_input,
    w_gate_out,
    forget_floor,
    group_gain,
    w_out,
    norm2_gain,
    ffn_gate,
    ffn_up,
    ffn_down,
    out_cotangent,
):
    row_count, shard_len, model_width = layer_input.shape
    assert row_count == 2 and size & (size - 1) == 0
    seq_len = doc_starts.shape[1]
    half_width = w_query.shape[1]
    half_heads = half_width // HEAD_DIM
    width = 2 * half_width
    me = lax.axis_index("head")
    place = lax.axis_index("dp")
    row = me % 2
    bits = [1 << at for at in range(1, size.bit_length() - 1)]
    own_tokens = 2 * shard_len
    hidden_dev = ffn_gate.shape[1]
    hidden_half = depth * hidden_dev

    def pick(tensor, at):
        return lax.dynamic_index_in_dim(tensor, at, 0, keepdims=False)

    def to_row(tensor):
        return jnp.concatenate((pick(tensor, row), swap(pick(tensor, 1 - row), 1, size)))

    def from_row(tensor):
        mine, other = tensor[:shard_len], swap(tensor[shard_len:], 1, size)
        return jnp.where(row == 0, jnp.stack((mine, other)), jnp.stack((other, mine)))

    two = len(bits) == 2

    def chunk(tensor, at):
        return tensor[at * own_tokens : (at + 1) * own_tokens]

    pair_rows = layer_input.astype(f32)
    pair_scale = rms_scale(pair_rows)
    pair_normed = (pair_rows * pair_scale * norm1_gain).astype(bf16)
    normed_mine, normed_theirs = pick(pair_normed, row), pick(pair_normed, 1 - row)
    gate_up, normed_mine, normed_theirs = tie((ffn_gate.T, ffn_up.T), normed_mine, normed_theirs)
    normed_sib = swap(normed_theirs, 1, size)
    if two:
        first, second = bits
        near_first = [swap(normed_mine, first, size), swap(normed_theirs, first | 1, size)]
        near_second = [swap(normed_mine, second, size), swap(normed_theirs, second | 1, size)]
        far = [swap(near_first[0], second, size), swap(near_second[1], first, size)]
        normed_parts = [normed_mine, normed_sib, *near_first, *near_second, *far]
    else:
        normed_parts = gather_start(jnp.concatenate((normed_mine, normed_sib)), bits, size)[1]

    normed_parts[1], out_cotangent = tie(normed_parts[1], out_cotangent)
    cot_own = to_row(out_cotangent)

    gate_up = lax.all_gather(jnp.stack(gate_up), "dp", axis=1, tiled=True)
    down = lax.all_gather(ffn_down.T, "dp", axis=0, tiled=True)

    proj_own = jnp.concatenate((w_query, w_forget, w_input, w_gate_out), axis=1)
    proj_weights = jnp.concatenate((proj_own, swap(proj_own, 1, size)), axis=1)
    vectors = jnp.stack((forget_floor, group_gain))
    vectors = jnp.concatenate((vectors, swap(vectors, 1, size)), axis=1)
    floor_row, gain_row = vectors[:1], vectors[1:]

    seg = jnp.cumsum(pick(doc_starts, row)).reshape(size, shard_len)
    seg_last = seg[:, -1]
    info = jnp.concatenate((me[None], jnp.zeros((1,), jnp.int32), seg_last[:-1], seg_last))
    seg = seg[:, None, :]

    proj = jnp.zeros((seq_len, 4 * width), f32)
    at = 0
    early = len(normed_parts) * 3 // 4 if two else 0
    for index, part in enumerate(normed_parts):
        if two and index == early:
            proj, *normed_parts[early:], cot_own, layer_input, w_out = tie(
                proj, *normed_parts[early:], cot_own, layer_input, w_out
            )
            part = normed_parts[index]
        proj = lax.dynamic_update_slice(proj, mm(part, proj_weights, NN), (at, 0))
        at += part.shape[0]
    gated, mixed, states, scores = recurrence(
        info, proj, floor_row, gain_row, seg, half_heads, size
    )
    out_weights = jnp.concatenate((w_out, swap(w_out, 1, size)))

    own_rows = to_row(layer_input)
    if two:
        cot_near = gather_near(cot_own, bits, size)
        gated, cot_near, own_rows = tie(gated, cot_near, own_rows)
    own_rows = own_rows.astype(f32)

    mixer_sum = Scatter(lambda at: mm(chunk(gated, at), out_weights, NN).astype(bf16), bits, size)
    resid = own_rows + mixer_sum.total(own_rows)[0]
    row_scale = rms_scale(resid)
    ffn_own = (resid * row_scale * norm2_gain).astype(bf16)
    ffn_own, gate_up = tie(ffn_own, gate_up)
    if two:
        ffn_near = gather_near(ffn_own, bits, size)
        ffn_near, cot_near = tie(ffn_near, cot_near)
        ffn_far = gather_far(ffn_near, bits, size)
        cot_flat = [cot_own, *cot_near, *gather_far(cot_near, bits, size)]
        ffn_parts = [ffn_own, *ffn_near, ffn_far]
    else:
        ffn_parts = gather_start(ffn_own, bits, size)[1]
        cot_flat = gather_start(cot_own, bits, size)[1]
    ffn_flat = [*ffn_parts[:3], *ffn_parts[3]] if two else ffn_parts
    count = len(ffn_parts)
    gate_rows, up_rows = stack_rows(gate_up, swap(gate_up, 1, size))

    gate_part, up_part, inner = [], [], []
    for at in range(count):
        if at:
            ffn_parts[at], inner[-1] = tie(ffn_parts[at], inner[-1])
        if two and at == 3:
            ffn_parts[3] = jnp.concatenate(ffn_parts[3])
        gate, up = mm(ffn_parts[at], gate_rows, NT), mm(ffn_parts[at], up_rows, NT)
        sig = jax.nn.sigmoid(gate)
        up_part.append(gate * sig)
        gate_part.append(up * sig * (1.0 + gate * (1.0 - sig)))
        inner.append((up_part[-1] * up).astype(bf16))
    lower, upper = (0, hidden_half), (hidden_half, hidden_half)
    down_other = cross([inner], cot_flat, left_cols=upper)
    down_other, inner[0], down = tie(down_other, inner[0], down)
    down_own = cross([inner], cot_flat, left_cols=lower)
    down_pair = add_pair(down_own[0], swap(down_other[0], 1, size))
    (down_rows,) = stack_rows(down[None], swap(down, 1, size)[None])
    down_pair, cot_flat = tie(down_pair, cot_flat)
    cot_parts = [*cot_flat[:3], jnp.concatenate(cot_flat[3:])] if two else cot_flat
    ffn_down_grad = lax.psum_scatter(down_pair, "dp", scatter_dimension=0, tiled=True)

    gate_grad, up_grad, totals = [None] * count, [None] * count, []

    def ffn_part(at):
        part = cot_parts[at]
        if totals:
            part, totals[-1] = tie(part, totals[-1])
        inner_grad = mm(part, down_rows, NT)
        gate_grad[at] = (inner_grad * gate_part[at]).astype(bf16)
        up_grad[at] = (inner_grad * up_part[at]).astype(bf16)
        totals.append(
            add(mm(gate_grad[at], gate_rows, NN), mm(up_grad[at], up_rows, NN)).astype(bf16)
        )
        return totals[-1]

    ffn_sum = Scatter(ffn_part, bits, size)
    if two:
        ffn_sum.own, gate_grad, up_grad = tie(ffn_sum.own, gate_grad, up_grad)
    gate_up_other = cross([gate_grad, up_grad], ffn_flat, left_cols=upper)
    if two:
        ffn_sum.moved, gate_up_other = tie(ffn_sum.moved, gate_up_other)
        ffn_sum.finish()
        ffn_sum.sends, gate_grad, up_grad = tie(ffn_sum.sends, gate_grad, up_grad)
    gate_up_other, gate_grad, up_grad, ffn_down_grad = tie(
        gate_up_other, gate_grad, up_grad, ffn_down_grad
    )
    gate_up_own = cross([gate_grad, up_grad], ffn_flat, left_cols=lower)
    gate_up_pair = add_pair(
        gate_up_own.reshape(-1, model_width), swap(gate_up_other, 1, size).reshape(-1, model_width)
    ).reshape(gate_up_own.shape)
    ffn_in_grad, gate_up_pair = ffn_sum.total(gate_up_pair)
    gate_up_grad = lax.psum_scatter(gate_up_pair, "dp", scatter_dimension=1, tiled=True)

    scaled = ffn_in_grad * norm2_gain
    resid_grad = cot_own.astype(f32) + row_scale * (
        scaled - resid * row_scale * row_scale * jnp.mean(scaled * resid, axis=-1, keepdims=True)
    )
    norm2_part = jnp.sum(ffn_in_grad * resid * row_scale, axis=0)
    mixer_parts = gather_start(resid_grad.astype(bf16), bits, size)[1]
    mixer_grad = jnp.concatenate(mixer_parts)

    out_other = cross([[gated]], mixer_parts, left_cols=(half_width, half_width))
    out_other, gated = tie(out_other, gated)
    out_own = cross([[gated]], mixer_parts, left_cols=(0, half_width))
    mixer_grad, out_own = tie(mixer_grad, out_own)
    out_pair = add_pair(out_own[0], swap(out_other[0], 1, size))
    gated_grad = mm(mixer_grad, out_weights, NT)
    proj_grad, floor_grad, gain_grad = recurrence_back(
        info, proj, floor_row, gain_row, seg, mixed, gated_grad, states, scores, half_heads, size
    )
    line = [proj_grad]

    def normed_part(at):
        part = mm(chunk(line[0], at), proj_weights, NT).astype(bf16)
        line[0], part = tie(line[0], part)
        return part

    normed_sum = Scatter(normed_part, bits, size)
    proj_grad = line[0]

    proj_other = cross([normed_parts], [proj_grad], right_cols=(2 * width, 2 * width))
    if two:
        normed_sum.at_first, normed_sum.at_second, proj_other = tie(
            normed_sum.at_first, normed_sum.at_second, proj_other
        )
        normed_sum.finish()
        normed_sum.sends, proj_grad = tie(normed_sum.sends, proj_grad)
    proj_grad, proj_other = tie(proj_grad, proj_other)
    proj_own = cross([normed_parts], [proj_grad], right_cols=(0, 2 * width))
    normed_grad, proj_own = normed_sum.total(proj_own)
    proj_pair = add_pair(proj_own[0], swap(proj_other[0], 1, size))
    proj_pair, out_pair, gate_up_grad = tie(proj_pair, out_pair, gate_up_grad)
    out_grad = lax.psum_scatter(out_pair, "dp", scatter_dimension=1, tiled=True)
    proj_w_grad = lax.psum_scatter(proj_pair, "dp", scatter_dimension=0, tiled=True).astype(f32)

    input_scale = rms_scale(own_rows)
    scaled_in = normed_grad * norm1_gain
    input_grad = resid_grad + input_scale * (
        scaled_in
        - own_rows
        * input_scale
        * input_scale
        * jnp.mean(scaled_in * own_rows, axis=-1, keepdims=True)
    )
    norm1_part = jnp.sum(normed_grad * own_rows * input_scale, axis=0)
    input_grad = from_row(input_grad)

    inner, norm1_part = tie(inner, norm1_part)
    output_sum = Scatter(lambda at: mm(inner[at], down_rows, NN).astype(bf16), bits, size)
    output = from_row(add(resid, output_sum.total(resid)[0]).astype(bf16))

    vector_grads = jnp.concatenate((gain_grad, floor_grad))
    vector_grads = vector_grads[:, :half_width] + swap(vector_grads[:, half_width:], 1, size)
    moved = [
        lax.ppermute(vector_grads, "dp", [(at, (at + slot) % depth) for at in range(depth)])
        for slot in range(1, depth)
    ]
    vector_grads = sum(moved, vector_grads)
    vector_len = half_width // depth
    vector_grads = lax.dynamic_slice_in_dim(vector_grads, place * vector_len, vector_len, 1)
    norm_grads = jnp.stack((norm1_part, norm2_part))
    for bit in [1] + bits:
        norm_grads = norm_grads + swap(norm_grads, bit, size)
    moved = [
        lax.ppermute(norm_grads, "dp", [(at, (at + slot) % depth) for at in range(depth)])
        for slot in range(1, depth)
    ]
    stacked = jnp.stack([norm_grads] + moved)
    order = (place - jnp.arange(depth)) % depth
    norm_grads = jnp.sum(jnp.zeros_like(stacked).at[order].set(stacked), axis=0)

    return (
        output,
        input_grad,
        proj_w_grad[:, 0:half_width],
        proj_w_grad[:, half_width : 2 * half_width],
        proj_w_grad[:, 2 * half_width : 3 * half_width],
        proj_w_grad[:, 3 * half_width : 4 * half_width],
        out_grad.astype(f32),
        vector_grads[0],
        vector_grads[1],
        norm_grads[0],
        norm_grads[1],
        gate_up_grad[0].astype(f32).T,
        gate_up_grad[1].astype(f32).T,
        ffn_down_grad.astype(f32).T,
    )


def solution(mesh):
    placed = (
        P("dp", "head", None),
        P("dp", None),
        P(),
        P(None, "head"),
        P(None, "head"),
        P(None, "head"),
        P(None, "head"),
        P("head"),
        P("head"),
        P("head", None),
        P(),
        P(None, ("head", "dp")),
        P(None, ("head", "dp")),
        P(None, ("head", "dp")),
        P("dp", "head", None),
    )
    return jax.shard_map(
        functools.partial(per_device, mesh.shape["head"], mesh.shape["dp"]),
        mesh=mesh,
        in_specs=placed,
        out_specs=(
            P("dp", "head", None),
            P("dp", "head", None),
            P("dp", "head"),
            P("dp", "head"),
            P("dp", "head"),
            P("dp", "head"),
            P("head", "dp"),
            P(("head", "dp")),
            P(("head", "dp")),
            P(),
            P(),
            P(None, ("head", "dp")),
            P(None, ("head", "dp")),
            P(None, ("head", "dp")),
        ),
        check_vma=False,
    )
```

```python
import functools

import jax
import jax.numpy as jnp
from jax import lax
from jax.experimental import pallas as pl
from jax.experimental.pallas import tpu as pltpu
from jax.sharding import PartitionSpec as P

HEAD_DIM = 128
epsilon = 1e-06
f32 = jnp.float32
bf16 = jnp.bfloat16


def swap(tensor, bit, size):
    return lax.ppermute(tensor, "head", [(at, at ^ bit) for at in range(size)])


def mm(left, right, dims, out=f32):
    return lax.dot_general(left, right, (dims, ((), ())), preferred_element_type=out)


NN = ((1,), (0,))
NT = ((1,), (1,))
TN = ((0,), (0,))


def rms_scale(tensor):
    return lax.rsqrt(jnp.mean(tensor * tensor, axis=-1, keepdims=True) + epsilon)


def gather_near(own, bits, size):
    return swap(own, bits[0], size), swap(own, bits[1], size)


def gather_far(near, bits, size):
    half = near[0].shape[0] // 2
    return swap(near[0][:half], bits[1], size), swap(near[1][half:], bits[0], size)


def gather_start(own, bits, size):
    if len(bits) == 2:
        near = gather_near(own, bits, size)
        return near, [own, *near, *gather_far(near, bits, size)]
    parts = [own]
    for bit in bits:
        moved = swap(jnp.stack(parts), bit, size)
        parts = parts + [moved[at] for at in range(len(parts))]
    return parts[1:], parts


class Scatter:
    def __init__(self, part_of, bits, size):
        self.bits, self.size = bits, size
        self.moved, self.sends = [], None
        if len(bits) == 2:
            first, second = bits
            both = part_of(3)
            self.half = half = both.shape[0] // 2
            top_both, bottom_both = swap(both[:half], first, size), swap(both[half:], second, size)
            self.at_first, self.at_second = part_of(1), part_of(2)
            top_first = swap(self.at_first[:half], first, size)
            bottom_second = swap(self.at_second[half:], second, size)
            self.moved = [top_both, bottom_both, top_first, bottom_second]
            self.own = part_of(0)
        else:
            self.parts = [part_of(at) for at in range(1 << len(bits))]

    def finish(self):
        self.moved = list(tie(*self.moved))
        top_both, bottom_both = self.moved[:2]
        self.sends = (
            add(self.at_first[self.half :], bottom_both).astype(bf16),
            add(self.at_second[: self.half], top_both).astype(bf16),
        )

    def total(self, held=None):
        bits, size = self.bits, self.size
        if len(bits) == 2:
            first, second = bits
            if self.sends is None:
                self.finish()
            bottom_first, top_second = swap(self.sends[0], first, size), swap(self.sends[1], second, size)
            bottom_first, top_second, held = tie(bottom_first, top_second, held)
            top_first, bottom_second = self.moved[2:]
            top = add(self.own[: self.half], top_first, top_second)
            bottom = add(self.own[self.half :], bottom_first, bottom_second)
            return jnp.concatenate((top, bottom)), held
        parts = [part.astype(f32) for part in self.parts]
        for bit in reversed(bits):
            count = len(parts) // 2
            moved = swap(jnp.stack(parts[count:]).astype(bf16), bit, size)
            parts = [add(parts[at], moved[at]) for at in range(count)]
        return parts[0], held


def add(first, *rest):
    total = first.astype(f32)
    for term in rest:
        total = total + term.astype(f32)
    return total


def tie(*tensors):
    return lax.optimization_barrier(tensors)


def halves(tensor):
    high = tensor.astype(bf16)
    return high, (tensor - high.astype(f32)).astype(bf16)


def cumulate(triangle, tensor):
    high, low = halves(tensor)
    return mm(triangle, high, NN) + mm(triangle, low, NN)


def span_masks(info, block, blocks, seg_ref):
    span = seg_ref.shape[-1]
    across = jnp.broadcast_to(seg_ref[0], (span, span))
    down = across.T
    rows = lax.broadcasted_iota(jnp.int32, (span, span), 0)
    cols = lax.broadcasted_iota(jnp.int32, (span, span), 1)
    before = info[1 + block]
    last = info[1 + blocks + block]
    same = (across == down) & (rows >= cols)
    column = down[:, :1]
    carried = (column == before).astype(f32)
    to_final = (column == last).astype(f32)
    through = (before == last).astype(f32)
    return rows, cols, same, carried, to_final, through


def head_columns(head, half_heads, half_width):
    base = (head // half_heads) * 4 * half_width + (head % half_heads) * HEAD_DIM
    return [slice(base + at * half_width, base + at * half_width + HEAD_DIM) for at in range(4)]


def forward_kernel(
    blocks, half_heads, info, proj_ref, floor_ref, gain_ref, seg_ref, gated_ref, mixed_ref, states_ref, scores_ref, state
):
    block = pl.program_id(0)
    half_width = half_heads * HEAD_DIM

    @pl.when(block == 0)
    def _():
        state[...] = jnp.zeros_like(state)

    rows, cols, same, carried, to_final, through = span_masks(info, block, blocks, seg_ref)
    span = rows.shape[0]
    lower = (rows >= cols).astype(bf16)
    for head in range(2 * half_heads):
        lanes = slice(head * HEAD_DIM, (head + 1) * HEAD_DIM)
        at_q, at_f, at_v, at_g = head_columns(head, half_heads, half_width)
        queries, forget_pre = proj_ref[:, at_q], proj_ref[:, at_f]
        values, gate = proj_ref[:, at_v].astype(bf16), proj_ref[:, at_g]
        inject = (1.0 - floor_ref[:, lanes]) / (1.0 + jnp.exp(forget_pre))
        decays = cumulate(lower, jnp.log(1.0 - inject))
        last = decays[span - 1 :, :]
        lifted, lifted_rest = halves(queries * jnp.exp(decays))
        lowered, lowered_rest = halves(inject * jnp.exp(-decays))
        scores = mm(lifted, lowered, NT) + mm(lifted, lowered_rest, NT) + mm(lifted_rest, lowered, NT)
        scores = jnp.where(same, scores, 0.0).astype(bf16)
        scores_ref[0, head] = scores
        now = state[head]
        states_ref[0, head] = now
        mixed = mm(scores, values, NN) + carried * mm(lifted, now.astype(bf16), NT)
        kept = (inject * jnp.exp(last - decays) * to_final).astype(bf16)
        state[head] = now * (jnp.exp(last) * through) + mm(values, kept, TN)
        mixed_ref[:, lanes] = mixed
        grouped = mixed * rms_scale(mixed) * gain_ref[:, lanes]
        gated_ref[:, lanes] = (grouped * gate / (1.0 + jnp.exp(-gate))).astype(bf16)


def backward_kernel(
    blocks, half_heads, info, proj_ref, floor_ref, gain_ref, seg_ref, mixed_ref, grad_ref, states_ref, scores_ref,
    proj_grad_ref, floor_grad_ref, gain_grad_ref, state_grad,
):
    step = pl.program_id(0)
    block = blocks - 1 - step
    half_width = half_heads * HEAD_DIM

    @pl.when(step == 0)
    def _():
        state_grad[...] = jnp.zeros_like(state_grad)
        floor_grad_ref[...] = jnp.zeros_like(floor_grad_ref)
        gain_grad_ref[...] = jnp.zeros_like(gain_grad_ref)

    rows, cols, same, carried, to_final, through = span_masks(info, block, blocks, seg_ref)
    span = rows.shape[0]
    lower = (rows >= cols).astype(bf16)
    upper = (rows <= cols).astype(bf16)
    is_last = lax.broadcasted_iota(jnp.int32, (span, 1), 0) == span - 1
    for head in range(2 * half_heads):
        lanes = slice(head * HEAD_DIM, (head + 1) * HEAD_DIM)
        at_q, at_f, at_v, at_g = head_columns(head, half_heads, half_width)
        queries, forget_pre = proj_ref[:, at_q], proj_ref[:, at_f]
        values, gate = proj_ref[:, at_v].astype(bf16), proj_ref[:, at_g]
        mixed, gain, grad = mixed_ref[:, lanes], gain_ref[:, lanes], grad_ref[:, lanes]
        gate_sig = 1.0 / (1.0 + jnp.exp(-gate))
        scale = rms_scale(mixed)
        unit = mixed * scale
        grouped_grad = grad * gate * gate_sig
        proj_grad_ref[:, at_g] = (
            grad * unit * gain * gate_sig * (1.0 + gate * (1.0 - gate_sig))
        ).astype(bf16)
        gain_grad_ref[:, lanes] += jnp.sum(grouped_grad * unit, axis=0, keepdims=True)
        unit_grad = grouped_grad * gain
        mixed_grad, mixed_rest = halves(
            scale * (unit_grad - unit * jnp.mean(unit_grad * unit, axis=-1, keepdims=True))
        )
        room = 1.0 - floor_ref[:, lanes]
        sig = 1.0 / (1.0 + jnp.exp(forget_pre))
        inject = room * sig
        decays = cumulate(lower, jnp.log(1.0 - inject))
        last = decays[span - 1 :, :]
        rise, fall, rest = jnp.exp(decays), jnp.exp(-decays), jnp.exp(last - decays) * to_final
        lifted = (queries * rise).astype(bf16)
        lowered = (inject * fall).astype(bf16)
        kept = (inject * rest).astype(bf16)
        scores = scores_ref[0, head]
        scores_grad = mm(mixed_grad, values, NT) + mm(mixed_rest, values, NT)
        scores_grad = jnp.where(same, scores_grad, 0.0).astype(bf16)
        now, after = states_ref[0, head], state_grad[head]
        after_low, now_low = after.astype(bf16), now.astype(bf16)
        state_part = mm(mixed_grad, now_low, NN) + mm(mixed_rest, now_low, NN)
        lifted_grad = mm(scores_grad, lowered, NN) + carried * state_part
        lowered_grad = mm(scores_grad, lifted, TN)
        kept_grad = mm(values, after_low, NN)
        value_grad = mm(scores, mixed_grad, TN) + mm(kept, after_low, NT)
        kept_term = kept_grad * kept.astype(f32)
        decay_grad = lifted_grad * lifted.astype(f32) - lowered_grad * lowered.astype(f32) - kept_term
        pass_on = jnp.exp(last) * through
        last_grad = jnp.sum(kept_term, axis=0, keepdims=True) + pass_on * jnp.sum(
            now * after, axis=0, keepdims=True
        )
        decay_grad = decay_grad + jnp.where(is_last, last_grad, 0.0)
        log_grad = cumulate(upper, decay_grad)
        inject_grad = lowered_grad * fall + kept_grad * rest - log_grad / (1.0 - inject)
        state_grad[head] = after * pass_on + mm(
            mixed_grad, (lifted.astype(f32) * carried).astype(bf16), TN
        )
        proj_grad_ref[:, at_q] = (lifted_grad * rise).astype(bf16)
        proj_grad_ref[:, at_f] = (-inject_grad * room * sig * (1.0 - sig)).astype(bf16)
        proj_grad_ref[:, at_v] = value_grad.astype(bf16)
        floor_grad_ref[:, lanes] -= jnp.sum(inject_grad * sig, axis=0, keepdims=True)


def recurrence(info, proj, floor_row, gain_row, seg, half_heads, size):
    blocks, _, span = seg.shape
    width = floor_row.shape[1]
    spot = lambda block, info: (block ^ info[0], 0)
    fixed = lambda block, info: (0, 0)
    return pl.pallas_call(
        functools.partial(forward_kernel, blocks, half_heads),
        out_shape=(
            jax.ShapeDtypeStruct((blocks * span, width), bf16),
            jax.ShapeDtypeStruct((blocks * span, width), f32),
            jax.ShapeDtypeStruct((blocks, 2 * half_heads, HEAD_DIM, HEAD_DIM), f32),
            jax.ShapeDtypeStruct((blocks, 2 * half_heads, span, span), bf16),
        ),
        grid_spec=pltpu.PrefetchScalarGridSpec(
            num_scalar_prefetch=1,
            grid=(blocks,),
            in_specs=[
                pl.BlockSpec((span, 4 * width), spot),
                pl.BlockSpec((1, width), fixed),
                pl.BlockSpec((1, width), fixed),
                pl.BlockSpec((1, 1, span), lambda block, info: (block, 0, 0)),
            ],
            out_specs=[
                pl.BlockSpec((span, width), spot),
                pl.BlockSpec((span, width), spot),
                pl.BlockSpec(
                    (1, 2 * half_heads, HEAD_DIM, HEAD_DIM), lambda block, info: (block, 0, 0, 0)
                ),
                pl.BlockSpec((1, 2 * half_heads, span, span), lambda block, info: (block, 0, 0, 0)),
            ],
            scratch_shapes=[pltpu.VMEM((2 * half_heads, HEAD_DIM, HEAD_DIM), f32)],
        ),
        compiler_params=pltpu.CompilerParams(vmem_limit_bytes=16 * 2**20),
        cost_estimate=pl.CostEstimate(
            flops=0, bytes_accessed=0, transcendentals=0
        ),
    )(info, proj, floor_row, gain_row, seg)


def recurrence_back(info, proj, floor_row, gain_row, seg, mixed, grad, states, scores, half_heads, size):
    blocks, _, span = seg.shape
    width = floor_row.shape[1]
    spot = lambda step, info: ((blocks - 1 - step) ^ info[0], 0)
    fixed = lambda step, info: (0, 0)
    return pl.pallas_call(
        functools.partial(backward_kernel, blocks, half_heads),
        out_shape=(
            jax.ShapeDtypeStruct((blocks * span, 4 * width), bf16),
            jax.ShapeDtypeStruct((1, width), f32),
            jax.ShapeDtypeStruct((1, width), f32),
        ),
        grid_spec=pltpu.PrefetchScalarGridSpec(
            num_scalar_prefetch=1,
            grid=(blocks,),
            in_specs=[
                pl.BlockSpec((span, 4 * width), spot),
                pl.BlockSpec((1, width), fixed),
                pl.BlockSpec((1, width), fixed),
                pl.BlockSpec((1, 1, span), lambda step, info: (blocks - 1 - step, 0, 0)),
                pl.BlockSpec((span, width), spot),
                pl.BlockSpec((span, width), spot),
                pl.BlockSpec(
                    (1, 2 * half_heads, HEAD_DIM, HEAD_DIM),
                    lambda step, info: (blocks - 1 - step, 0, 0, 0),
                ),
                pl.BlockSpec(
                    (1, 2 * half_heads, span, span), lambda step, info: (blocks - 1 - step, 0, 0, 0)
                ),
            ],
            out_specs=[
                pl.BlockSpec((span, 4 * width), spot),
                pl.BlockSpec((1, width), fixed),
                pl.BlockSpec((1, width), fixed),
            ],
            scratch_shapes=[pltpu.VMEM((2 * half_heads, HEAD_DIM, HEAD_DIM), f32)],
        ),
        compiler_params=pltpu.CompilerParams(vmem_limit_bytes=20 * 2**20),
        cost_estimate=pl.CostEstimate(
            flops=0, bytes_accessed=0, transcendentals=0
        ),
    )(info, proj, floor_row, gain_row, seg, mixed, grad, states, scores)


def stack_kernel(count, own, other, *refs):
    outs, sems = refs[:count], refs[count]
    half = own.shape[1]
    copies = []
    for at in range(count):
        for side, source in enumerate((own, other)):
            target = outs[at].at[pl.ds(side * half, half)]
            copies.append(pltpu.make_async_copy(source.at[at], target, sems.at[at, side]))
    for copy in copies:
        copy.start()
    for copy in copies:
        copy.wait()


def stack_rows(own, other):
    count, rows, depth = own.shape
    return pl.pallas_call(
        functools.partial(stack_kernel, count),
        out_shape=[jax.ShapeDtypeStruct((2 * rows, depth), own.dtype)] * count,
        in_specs=[pl.BlockSpec(memory_space=pl.ANY)] * 2,
        out_specs=[pl.BlockSpec(memory_space=pltpu.VMEM)] * count,
        scratch_shapes=[pltpu.SemaphoreType.DMA((count, 2))],
        compiler_params=pltpu.CompilerParams(vmem_limit_bytes=4 * 2**20),
        cost_estimate=pl.CostEstimate(flops=0, bytes_accessed=0, transcendentals=0),
    )(own, other)


def free_call(kernel, out_shape, megabytes, *args):
    vmem = pl.BlockSpec(memory_space=pltpu.VMEM)
    return pl.pallas_call(
        kernel,
        out_shape=out_shape,
        in_specs=[vmem] * len(args),
        out_specs=jax.tree.map(lambda _: vmem, out_shape),
        compiler_params=pltpu.CompilerParams(vmem_limit_bytes=megabytes * 2**20),
        cost_estimate=pl.CostEstimate(flops=0, bytes_accessed=0, transcendentals=0),
    )(*args)


def add_kernel(count, *refs):
    out = refs[-1]
    rows = refs[0].shape[0]
    step = 64 if rows % 64 == 0 else rows
    for at in range(count):
        for row in range(0, rows, step):
            here = slice(row, row + step)
            left, right = refs[2 * at][here], refs[2 * at + 1][here]
            out[at, here] = (left.astype(f32) + right.astype(f32)).astype(bf16)


def add_pairs(*pairs):
    out = jax.ShapeDtypeStruct((len(pairs),) + pairs[0][0].shape, bf16)
    args = [one for pair in pairs for one in pair]
    return free_call(functools.partial(add_kernel, len(pairs)), out, 8, *args)


def pieces(lefts, rights):
    found, left, right, start, begin = [], 0, 0, 0, 0
    while left < len(lefts):
        rows = min(lefts[left].shape[0] - start, rights[right].shape[0] - begin)
        found.append(((lefts[left], start), (rights[right], begin), rows))
        start, begin = start + rows, begin + rows
        if start == lefts[left].shape[0]:
            left, start = left + 1, 0
        if begin == rights[right].shape[0]:
            right, begin = right + 1, 0
    return found


def cross_kernel(count, by_rows, *refs):
    own, other = refs[-2:]
    rows = refs[0].shape[1]
    width = refs[count].shape[1]
    step = 512 if rows < 2048 else 256
    step = step if (width if by_rows else width // 2) % step == 0 else width // 2
    found = pieces(refs[:count], refs[count:-2])
    for col in range(0, width, step):
        lanes = slice(col, col + step)
        total, lefts, rights, held = None, [], [], 0
        for index, ((one, start), (two, begin), tokens) in enumerate(found):
            lefts.append(one[start : start + tokens])
            rights.append(two[begin : begin + tokens, lanes])
            held += tokens
            if held >= 256 or index == len(found) - 1:
                left = lefts[0] if len(lefts) == 1 else jnp.concatenate(lefts)
                right = rights[0] if len(rights) == 1 else jnp.concatenate(rights)
                term = mm(left, right, TN)
                total = term if total is None else total + term
                lefts, rights, held = [], [], 0
        if by_rows:
            own[:, lanes] = total[: rows // 2].astype(bf16)
            other[:, lanes] = total[rows // 2 :].astype(bf16)
        elif col < width // 2:
            own[:, lanes] = total.astype(bf16)
        else:
            other[:, col - width // 2 : col - width // 2 + step] = total.astype(bf16)


def cross(lefts, rights, by_rows=True):
    rows, width = lefts[0].shape[1], rights[0].shape[1]
    half = (rows // 2, width) if by_rows else (rows, width // 2)
    out = [jax.ShapeDtypeStruct(half, bf16)] * 2
    return free_call(functools.partial(cross_kernel, len(lefts), by_rows), out, 10, *lefts, *rights)


def per_device(
    size,
    depth,
    layer_input,
    doc_starts,
    norm1_gain,
    w_query,
    w_forget,
    w_input,
    w_gate_out,
    forget_floor,
    group_gain,
    w_out,
    norm2_gain,
    ffn_gate,
    ffn_up,
    ffn_down,
    out_cotangent,
):
    row_count, shard_len, model_width = layer_input.shape
    assert row_count == 2 and size & (size - 1) == 0
    seq_len = doc_starts.shape[1]
    half_width = w_query.shape[1]
    half_heads = half_width // HEAD_DIM
    width = 2 * half_width
    me = lax.axis_index("head")
    place = lax.axis_index("dp")
    row = me % 2
    bits = [1 << at for at in range(1, size.bit_length() - 1)]
    own_tokens = 2 * shard_len
    hidden_dev = ffn_gate.shape[1]
    hidden_half = depth * hidden_dev

    def pick(tensor, at):
        return lax.dynamic_index_in_dim(tensor, at, 0, keepdims=False)

    def to_row(tensor):
        return jnp.concatenate((pick(tensor, row), swap(pick(tensor, 1 - row), 1, size)))

    def from_row(tensor):
        mine, other = tensor[:shard_len], swap(tensor[shard_len:], 1, size)
        return jnp.where(row == 0, jnp.stack((mine, other)), jnp.stack((other, mine)))

    two = len(bits) == 2

    def chunk(tensor, at):
        return tensor[at * own_tokens : (at + 1) * own_tokens]

    pair_rows = layer_input.astype(f32)
    pair_scale = rms_scale(pair_rows)
    pair_normed = (pair_rows * pair_scale * norm1_gain).astype(bf16)
    normed_mine, normed_theirs = pick(pair_normed, row), pick(pair_normed, 1 - row)
    gate_up, normed_mine, normed_theirs = tie((ffn_gate.T, ffn_up.T), normed_mine, normed_theirs)
    normed_sib = swap(normed_theirs, 1, size)
    if two:
        first, second = bits
        near_first = [swap(normed_mine, first, size), swap(normed_theirs, first | 1, size)]
        near_second = [swap(normed_mine, second, size), swap(normed_theirs, second | 1, size)]
        far = [swap(near_first[0], second, size), swap(near_second[1], first, size)]
        normed_parts = [normed_mine, normed_sib, *near_first, *near_second, *far]
    else:
        normed_parts = gather_start(jnp.concatenate((normed_mine, normed_sib)), bits, size)[1]

    normed_parts[1], out_cotangent = tie(normed_parts[1], out_cotangent)
    cot_own = to_row(out_cotangent)

    gate_up = lax.all_gather(jnp.stack(gate_up), "dp", axis=1, tiled=True)
    down = lax.all_gather(ffn_down.T, "dp", axis=0, tiled=True)

    proj_own = jnp.concatenate((w_query, w_forget, w_input, w_gate_out), axis=1)
    proj_weights = jnp.concatenate((proj_own, swap(proj_own, 1, size)), axis=1)
    vectors = jnp.stack((forget_floor, group_gain))
    vectors = jnp.concatenate((vectors, swap(vectors, 1, size)), axis=1)
    floor_row, gain_row = vectors[:1], vectors[1:]

    seg = jnp.cumsum(pick(doc_starts, row)).reshape(size, shard_len)
    seg_last = seg[:, -1]
    info = jnp.concatenate((me[None], jnp.zeros((1,), jnp.int32), seg_last[:-1], seg_last))
    seg = seg[:, None, :]

    proj = jnp.zeros((seq_len, 4 * width), f32)
    at = 0
    early = len(normed_parts) * 3 // 4 if two else 0
    for index, part in enumerate(normed_parts):
        if two and index == early:
            proj, *normed_parts[early:], cot_own, layer_input, w_out = tie(
                proj, *normed_parts[early:], cot_own, layer_input, w_out
            )
            part = normed_parts[index]
        if two and index >= early:
            if index == early:
                continue
            part = jnp.concatenate(normed_parts[early:])
        proj = lax.dynamic_update_slice(proj, mm(part, proj_weights, NN), (at, 0))
        at += part.shape[0]
    gated, mixed, states, scores = recurrence(
        info, proj, floor_row, gain_row, seg, half_heads, size
    )
    out_weights = jnp.concatenate((w_out, swap(w_out, 1, size)))

    own_rows = to_row(layer_input)
    if two:
        cot_near = gather_near(cot_own, bits, size)
        gated, cot_near, own_rows = tie(gated, cot_near, own_rows)
    own_rows = own_rows.astype(f32)

    mixer_sum = Scatter(lambda at: mm(chunk(gated, at), out_weights, NN).astype(bf16), bits, size)
    resid = own_rows + mixer_sum.total(own_rows)[0]
    row_scale = rms_scale(resid)
    ffn_own = (resid * row_scale * norm2_gain).astype(bf16)
    ffn_own, gate_up = tie(ffn_own, gate_up)
    if two:
        ffn_near = gather_near(ffn_own, bits, size)
        ffn_near, cot_near = tie(ffn_near, cot_near)
        ffn_far = gather_far(ffn_near, bits, size)
        cot_flat = [cot_own, *cot_near, *gather_far(cot_near, bits, size)]
        ffn_parts = [ffn_own, *ffn_near, ffn_far]
    else:
        ffn_parts = gather_start(ffn_own, bits, size)[1]
        cot_flat = gather_start(cot_own, bits, size)[1]
    ffn_flat = [*ffn_parts[:3], *ffn_parts[3]] if two else ffn_parts
    count = len(ffn_parts)
    gate_rows, up_rows = stack_rows(gate_up, swap(gate_up, 1, size))

    gate_part, up_part, inner = [], [], []
    for at in range(count):
        if at:
            ffn_parts[at], inner[-1] = tie(ffn_parts[at], inner[-1])
        if at == count - 1:
            ffn_parts[at], cot_flat = tie(ffn_parts[at], cot_flat)
        if two and at == 3:
            ffn_parts[3] = jnp.concatenate(ffn_parts[3])
        gate, up = mm(ffn_parts[at], gate_rows, NT), mm(ffn_parts[at], up_rows, NT)
        sig = jax.nn.sigmoid(gate)
        silu = gate * sig
        up_part.append(silu.astype(bf16))
        gate_part.append((up * sig * (1.0 + gate * (1.0 - sig))).astype(bf16))
        inner.append((silu * up).astype(bf16))
    inner[-1], down = tie(inner[-1], down)
    down_own, down_other = cross(inner, cot_flat)
    down_received, down_own = tie(swap(down, 1, size), down_own)
    down_other = swap(down_other, 1, size)
    down_pair = None
    (down_rows,) = stack_rows(down[None], down_received[None])
    cot_parts = [*cot_flat[:3], jnp.concatenate(cot_flat[3:])] if two else cot_flat
    gate_grad, up_grad, totals = [None] * count, [None] * count, []

    def ffn_part(at):
        nonlocal down_other, down_pair
        part = cot_parts[at]
        if len(totals) == 1:
            down_other, totals[0] = tie(down_other, totals[0])
            down_pair = add_pairs((down_own, down_other))[0]
            part, down_pair = tie(part, down_pair)
        if totals:
            part, totals[-1] = tie(part, totals[-1])
        inner_grad = mm(part, down_rows, NT)
        gate_grad[at] = (inner_grad * gate_part[at].astype(f32)).astype(bf16)
        up_grad[at] = (inner_grad * up_part[at].astype(f32)).astype(bf16)
        totals.append(
            add(mm(gate_grad[at], gate_rows, NN), mm(up_grad[at], up_rows, NN)).astype(bf16)
        )
        return totals[-1]

    ffn_sum = Scatter(ffn_part, bits, size)
    ffn_down_grad = lax.psum_scatter(down_pair, "dp", scatter_dimension=0, tiled=True)
    if two:
        ffn_sum.own, gate_grad[0] = tie(ffn_sum.own, gate_grad[0])
    gate_own, gate_other = cross(gate_grad, ffn_flat)
    gate_other, up_grad[0] = tie(gate_other, up_grad[0])
    up_own, up_other = cross(up_grad, ffn_flat)
    up_other, ffn_down_grad = tie(up_other, ffn_down_grad)
    if two:
        ffn_sum.moved, up_other = tie(ffn_sum.moved, up_other)
        ffn_sum.finish()
    gate_up_pair = add_pairs(
        (gate_own, swap(gate_other, 1, size)), (up_own, swap(up_other, 1, size))
    )
    ffn_in_grad = ffn_sum.total(resid)[0]
    gate_up_grad = lax.psum_scatter(gate_up_pair, "dp", scatter_dimension=1, tiled=True)

    scaled = ffn_in_grad * norm2_gain
    resid_grad = cot_own.astype(f32) + row_scale * (
        scaled - resid * row_scale * row_scale * jnp.mean(scaled * resid, axis=-1, keepdims=True)
    )
    norm2_part = jnp.sum(ffn_in_grad * resid * row_scale, axis=0)
    mixer_parts = gather_start(resid_grad.astype(bf16), bits, size)[1]
    output_parts = [mm(inner[at], down_rows, NN).astype(bf16) for at in range(count)]
    output_parts, mixer_parts[-1] = tie(output_parts, mixer_parts[-1])
    output_sum = Scatter(lambda at: output_parts[at], bits, size)
    mixer_grad = jnp.concatenate(mixer_parts)

    out_own, out_other = cross([gated], mixer_parts)
    mixer_grad, out_other = tie(mixer_grad, out_other)
    out_pair = add_pairs((out_own, swap(out_other, 1, size)))[0]
    gated_grad = mm(mixer_grad, out_weights, NT)
    proj_grad, floor_grad, gain_grad = recurrence_back(
        info, proj, floor_row, gain_row, seg, mixed, gated_grad, states, scores, half_heads, size
    )
    if two:
        output_sum.moved, proj_grad = tie(output_sum.moved, proj_grad)

    proj_own, proj_other = cross(normed_parts, [proj_grad], by_rows=False)
    proj_other, proj_grad = tie(proj_other, proj_grad)
    normed_all = mm(proj_grad, proj_weights, NT).astype(bf16)
    proj_other, normed_all = tie(swap(proj_other, 1, size), normed_all)
    proj_pair = add_pairs((proj_own, proj_other))[0]
    normed_sum = Scatter(lambda at: chunk(normed_all, at), bits, size)
    if two:
        normed_sum.finish()
    normed_grad = normed_sum.total(proj_own)[0]
    out_pair, gate_up_grad = tie(out_pair, gate_up_grad)
    out_grad = lax.psum_scatter(out_pair, "dp", scatter_dimension=1, tiled=True)
    proj_pair, out_grad = tie(proj_pair, out_grad)
    proj_w_grad = lax.psum_scatter(proj_pair, "dp", scatter_dimension=0, tiled=True).astype(f32)

    input_scale = rms_scale(own_rows)
    scaled_in = normed_grad * norm1_gain
    input_grad = resid_grad + input_scale * (
        scaled_in
        - own_rows
        * input_scale
        * input_scale
        * jnp.mean(scaled_in * own_rows, axis=-1, keepdims=True)
    )
    norm1_part = jnp.sum(normed_grad * own_rows * input_scale, axis=0)
    input_grad = from_row(input_grad)

    if two:
        output_sum.finish()
        output_sum.sends, norm1_part = tie(output_sum.sends, norm1_part)
    output = from_row(add(resid, output_sum.total(resid)[0]).astype(bf16))

    vector_grads = jnp.concatenate((gain_grad, floor_grad))
    vector_grads = vector_grads[:, :half_width] + swap(vector_grads[:, half_width:], 1, size)
    moved = [
        lax.ppermute(vector_grads, "dp", [(at, (at + slot) % depth) for at in range(depth)])
        for slot in range(1, depth)
    ]
    vector_grads = sum(moved, vector_grads)
    vector_len = half_width // depth
    vector_grads = lax.dynamic_slice_in_dim(vector_grads, place * vector_len, vector_len, 1)
    norm_grads = jnp.stack((norm1_part, norm2_part))
    for bit in [1] + bits:
        norm_grads = norm_grads + swap(norm_grads, bit, size)
    moved = [
        lax.ppermute(norm_grads, "dp", [(at, (at + slot) % depth) for at in range(depth)])
        for slot in range(1, depth)
    ]
    stacked = jnp.stack([norm_grads] + moved)
    order = (place - jnp.arange(depth)) % depth
    norm_grads = jnp.sum(jnp.zeros_like(stacked).at[order].set(stacked), axis=0)

    return (
        output,
        input_grad,
        proj_w_grad[:, 0:half_width],
        proj_w_grad[:, half_width : 2 * half_width],
        proj_w_grad[:, 2 * half_width : 3 * half_width],
        proj_w_grad[:, 3 * half_width : 4 * half_width],
        out_grad.astype(f32),
        vector_grads[0],
        vector_grads[1],
        norm_grads[0],
        norm_grads[1],
        gate_up_grad[0].astype(f32).T,
        gate_up_grad[1].astype(f32).T,
        ffn_down_grad.astype(f32).T,
    )


def solution(mesh):
    placed = (
        P("dp", "head", None),
        P("dp", None),
        P(),
        P(None, "head"),
        P(None, "head"),
        P(None, "head"),
        P(None, "head"),
        P("head"),
        P("head"),
        P("head", None),
        P(),
        P(None, ("head", "dp")),
        P(None, ("head", "dp")),
        P(None, ("head", "dp")),
        P("dp", "head", None),
    )
    return jax.shard_map(
        functools.partial(per_device, mesh.shape["head"], mesh.shape["dp"]),
        mesh=mesh,
        in_specs=placed,
        out_specs=(
            P("dp", "head", None),
            P("dp", "head", None),
            P("dp", "head"),
            P("dp", "head"),
            P("dp", "head"),
            P("dp", "head"),
            P("head", "dp"),
            P(("head", "dp")),
            P(("head", "dp")),
            P(),
            P(),
            P(None, ("head", "dp")),
            P(None, ("head", "dp")),
            P(None, ("head", "dp")),
        ),
        check_vma=False,
    )
```

```python
import functools

import jax
import jax.numpy as jnp
from jax import lax
from jax.experimental import pallas as pl
from jax.experimental.pallas import tpu as pltpu
from jax.sharding import PartitionSpec as P

HEAD_DIM = 128
epsilon = 1e-06
f32 = jnp.float32
bf16 = jnp.bfloat16


def swap(tensor, bit, size):
    return lax.ppermute(tensor, "head", [(at, at ^ bit) for at in range(size)])


def mm(left, right, dims, out=f32):
    return lax.dot_general(left, right, (dims, ((), ())), preferred_element_type=out)


NN = ((1,), (0,))
NT = ((1,), (1,))
TN = ((0,), (0,))


def rms_scale(tensor):
    return lax.rsqrt(jnp.mean(tensor * tensor, axis=-1, keepdims=True) + epsilon)


def gather_near(own, bits, size):
    return swap(own, bits[0], size), swap(own, bits[1], size)


def gather_far(near, bits, size):
    half = near[0].shape[0] // 2
    return swap(near[0][:half], bits[1], size), swap(near[1][half:], bits[0], size)


def gather_start(own, bits, size):
    if len(bits) == 2:
        near = gather_near(own, bits, size)
        return near, [own, *near, *gather_far(near, bits, size)]
    parts = [own]
    for bit in bits:
        moved = swap(jnp.stack(parts), bit, size)
        parts = parts + [moved[at] for at in range(len(parts))]
    return parts[1:], parts


class Scatter:
    def __init__(self, part_of, bits, size):
        self.bits, self.size = bits, size
        self.moved, self.sends = [], None
        if len(bits) == 2:
            first, second = bits
            both = part_of(3)
            self.half = half = both.shape[0] // 2
            top_both, bottom_both = swap(both[:half], first, size), swap(both[half:], second, size)
            self.at_first, self.at_second = part_of(1), part_of(2)
            top_first = swap(self.at_first[:half], first, size)
            bottom_second = swap(self.at_second[half:], second, size)
            self.moved = [top_both, bottom_both, top_first, bottom_second]
            self.own = part_of(0)
        else:
            self.parts = [part_of(at) for at in range(1 << len(bits))]

    def finish(self):
        self.moved = list(tie(*self.moved))
        top_both, bottom_both = self.moved[:2]
        self.sends = (
            add(self.at_first[self.half :], bottom_both).astype(bf16),
            add(self.at_second[: self.half], top_both).astype(bf16),
        )

    def total(self, held=None):
        bits, size = self.bits, self.size
        if len(bits) == 2:
            first, second = bits
            if self.sends is None:
                self.finish()
            bottom_first, top_second = swap(self.sends[0], first, size), swap(self.sends[1], second, size)
            bottom_first, top_second, held = tie(bottom_first, top_second, held)
            top_first, bottom_second = self.moved[2:]
            top = add(self.own[: self.half], top_first, top_second)
            bottom = add(self.own[self.half :], bottom_first, bottom_second)
            return jnp.concatenate((top, bottom)), held
        parts = [part.astype(f32) for part in self.parts]
        for bit in reversed(bits):
            count = len(parts) // 2
            moved = swap(jnp.stack(parts[count:]).astype(bf16), bit, size)
            parts = [add(parts[at], moved[at]) for at in range(count)]
        return parts[0], held


def add(first, *rest):
    total = first.astype(f32)
    for term in rest:
        total = total + term.astype(f32)
    return total


def tie(*tensors):
    return lax.optimization_barrier(tensors)


def halves(tensor):
    high = tensor.astype(bf16)
    return high, (tensor - high.astype(f32)).astype(bf16)


def cumulate(triangle, tensor):
    high, low = halves(tensor)
    return mm(triangle, high, NN) + mm(triangle, low, NN)


def span_masks(info, block, blocks, seg_ref):
    span = seg_ref.shape[-1]
    across = jnp.broadcast_to(seg_ref[0], (span, span))
    down = across.T
    rows = lax.broadcasted_iota(jnp.int32, (span, span), 0)
    cols = lax.broadcasted_iota(jnp.int32, (span, span), 1)
    before = info[1 + block]
    last = info[1 + blocks + block]
    same = (across == down) & (rows >= cols)
    column = down[:, :1]
    carried = (column == before).astype(f32)
    to_final = (column == last).astype(f32)
    through = (before == last).astype(f32)
    return rows, cols, same, carried, to_final, through


def head_columns(head, half_heads, half_width):
    base = (head // half_heads) * 4 * half_width + (head % half_heads) * HEAD_DIM
    return [slice(base + at * half_width, base + at * half_width + HEAD_DIM) for at in range(4)]


def forward_kernel(
    blocks, half_heads, info, proj_ref, floor_ref, gain_ref, seg_ref, gated_ref, mixed_ref, states_ref, scores_ref, state
):
    block = pl.program_id(0)
    half_width = half_heads * HEAD_DIM

    @pl.when(block == 0)
    def _():
        state[...] = jnp.zeros_like(state)

    rows, cols, same, carried, to_final, through = span_masks(info, block, blocks, seg_ref)
    span = rows.shape[0]
    lower = (rows >= cols).astype(bf16)
    for head in range(2 * half_heads):
        lanes = slice(head * HEAD_DIM, (head + 1) * HEAD_DIM)
        at_q, at_f, at_v, at_g = head_columns(head, half_heads, half_width)
        queries, forget_pre = proj_ref[:, at_q], proj_ref[:, at_f]
        values, gate = proj_ref[:, at_v].astype(bf16), proj_ref[:, at_g]
        inject = (1.0 - floor_ref[:, lanes]) / (1.0 + jnp.exp(forget_pre))
        decays = cumulate(lower, jnp.log(1.0 - inject))
        last = decays[span - 1 :, :]
        lifted, lifted_rest = halves(queries * jnp.exp(decays))
        lowered, lowered_rest = halves(inject * jnp.exp(-decays))
        scores = mm(lifted, lowered, NT) + mm(lifted, lowered_rest, NT) + mm(lifted_rest, lowered, NT)
        scores = jnp.where(same, scores, 0.0).astype(bf16)
        scores_ref[0, head] = scores
        now = state[head]
        states_ref[0, head] = now
        mixed = mm(scores, values, NN) + carried * mm(lifted, now.astype(bf16), NT)
        kept = (inject * jnp.exp(last - decays) * to_final).astype(bf16)
        state[head] = now * (jnp.exp(last) * through) + mm(values, kept, TN)
        mixed_ref[:, lanes] = mixed
        grouped = mixed * rms_scale(mixed) * gain_ref[:, lanes]
        gated_ref[:, lanes] = (grouped * gate / (1.0 + jnp.exp(-gate))).astype(bf16)


def backward_kernel(
    blocks, half_heads, info, proj_ref, floor_ref, gain_ref, seg_ref, mixed_ref, grad_ref, states_ref, scores_ref,
    proj_grad_ref, floor_grad_ref, gain_grad_ref, state_grad,
):
    step = pl.program_id(0)
    block = blocks - 1 - step
    half_width = half_heads * HEAD_DIM

    @pl.when(step == 0)
    def _():
        state_grad[...] = jnp.zeros_like(state_grad)
        floor_grad_ref[...] = jnp.zeros_like(floor_grad_ref)
        gain_grad_ref[...] = jnp.zeros_like(gain_grad_ref)

    rows, cols, same, carried, to_final, through = span_masks(info, block, blocks, seg_ref)
    span = rows.shape[0]
    lower = (rows >= cols).astype(bf16)
    upper = (rows <= cols).astype(bf16)
    is_last = lax.broadcasted_iota(jnp.int32, (span, 1), 0) == span - 1
    for head in range(2 * half_heads):
        lanes = slice(head * HEAD_DIM, (head + 1) * HEAD_DIM)
        at_q, at_f, at_v, at_g = head_columns(head, half_heads, half_width)
        queries, forget_pre = proj_ref[:, at_q], proj_ref[:, at_f]
        values, gate = proj_ref[:, at_v].astype(bf16), proj_ref[:, at_g]
        mixed, gain, grad = mixed_ref[:, lanes], gain_ref[:, lanes], grad_ref[:, lanes]
        gate_sig = 1.0 / (1.0 + jnp.exp(-gate))
        scale = rms_scale(mixed)
        unit = mixed * scale
        grouped_grad = grad * gate * gate_sig
        proj_grad_ref[:, at_g] = (
            grad * unit * gain * gate_sig * (1.0 + gate * (1.0 - gate_sig))
        ).astype(bf16)
        gain_grad_ref[:, lanes] += jnp.sum(grouped_grad * unit, axis=0, keepdims=True)
        unit_grad = grouped_grad * gain
        mixed_grad, mixed_rest = halves(
            scale * (unit_grad - unit * jnp.mean(unit_grad * unit, axis=-1, keepdims=True))
        )
        room = 1.0 - floor_ref[:, lanes]
        sig = 1.0 / (1.0 + jnp.exp(forget_pre))
        inject = room * sig
        decays = cumulate(lower, jnp.log(1.0 - inject))
        last = decays[span - 1 :, :]
        rise, fall, rest = jnp.exp(decays), jnp.exp(-decays), jnp.exp(last - decays) * to_final
        lifted = (queries * rise).astype(bf16)
        lowered = (inject * fall).astype(bf16)
        kept = (inject * rest).astype(bf16)
        scores = scores_ref[0, head]
        scores_grad = mm(mixed_grad, values, NT) + mm(mixed_rest, values, NT)
        scores_grad = jnp.where(same, scores_grad, 0.0).astype(bf16)
        now, after = states_ref[0, head], state_grad[head]
        after_low, now_low = after.astype(bf16), now.astype(bf16)
        state_part = mm(mixed_grad, now_low, NN) + mm(mixed_rest, now_low, NN)
        lifted_grad = mm(scores_grad, lowered, NN) + carried * state_part
        lowered_grad = mm(scores_grad, lifted, TN)
        kept_grad = mm(values, after_low, NN)
        value_grad = mm(scores, mixed_grad, TN) + mm(kept, after_low, NT)
        kept_term = kept_grad * kept.astype(f32)
        decay_grad = lifted_grad * lifted.astype(f32) - lowered_grad * lowered.astype(f32) - kept_term
        pass_on = jnp.exp(last) * through
        last_grad = jnp.sum(kept_term, axis=0, keepdims=True) + pass_on * jnp.sum(
            now * after, axis=0, keepdims=True
        )
        decay_grad = decay_grad + jnp.where(is_last, last_grad, 0.0)
        log_grad = cumulate(upper, decay_grad)
        inject_grad = lowered_grad * fall + kept_grad * rest - log_grad / (1.0 - inject)
        state_grad[head] = after * pass_on + mm(
            mixed_grad, (lifted.astype(f32) * carried).astype(bf16), TN
        )
        proj_grad_ref[:, at_q] = (lifted_grad * rise).astype(bf16)
        proj_grad_ref[:, at_f] = (-inject_grad * room * sig * (1.0 - sig)).astype(bf16)
        proj_grad_ref[:, at_v] = value_grad.astype(bf16)
        floor_grad_ref[:, lanes] -= jnp.sum(inject_grad * sig, axis=0, keepdims=True)


def recurrence(info, proj, floor_row, gain_row, seg, half_heads, size):
    blocks, _, span = seg.shape
    width = floor_row.shape[1]
    spot = lambda block, info: (block ^ info[0], 0)
    fixed = lambda block, info: (0, 0)
    return pl.pallas_call(
        functools.partial(forward_kernel, blocks, half_heads),
        out_shape=(
            jax.ShapeDtypeStruct((blocks * span, width), bf16),
            jax.ShapeDtypeStruct((blocks * span, width), f32),
            jax.ShapeDtypeStruct((blocks, 2 * half_heads, HEAD_DIM, HEAD_DIM), f32),
            jax.ShapeDtypeStruct((blocks, 2 * half_heads, span, span), bf16),
        ),
        grid_spec=pltpu.PrefetchScalarGridSpec(
            num_scalar_prefetch=1,
            grid=(blocks,),
            in_specs=[
                pl.BlockSpec((span, 4 * width), spot),
                pl.BlockSpec((1, width), fixed),
                pl.BlockSpec((1, width), fixed),
                pl.BlockSpec((1, 1, span), lambda block, info: (block, 0, 0)),
            ],
            out_specs=[
                pl.BlockSpec((span, width), spot),
                pl.BlockSpec((span, width), spot),
                pl.BlockSpec(
                    (1, 2 * half_heads, HEAD_DIM, HEAD_DIM), lambda block, info: (block, 0, 0, 0)
                ),
                pl.BlockSpec((1, 2 * half_heads, span, span), lambda block, info: (block, 0, 0, 0)),
            ],
            scratch_shapes=[pltpu.VMEM((2 * half_heads, HEAD_DIM, HEAD_DIM), f32)],
        ),
        compiler_params=pltpu.CompilerParams(vmem_limit_bytes=16 * 2**20),
        cost_estimate=pl.CostEstimate(
            flops=0, bytes_accessed=0, transcendentals=0
        ),
    )(info, proj, floor_row, gain_row, seg)


def recurrence_back(info, proj, floor_row, gain_row, seg, mixed, grad, states, scores, half_heads, size):
    blocks, _, span = seg.shape
    width = floor_row.shape[1]
    spot = lambda step, info: ((blocks - 1 - step) ^ info[0], 0)
    fixed = lambda step, info: (0, 0)
    return pl.pallas_call(
        functools.partial(backward_kernel, blocks, half_heads),
        out_shape=(
            jax.ShapeDtypeStruct((blocks * span, 4 * width), bf16),
            jax.ShapeDtypeStruct((1, width), f32),
            jax.ShapeDtypeStruct((1, width), f32),
        ),
        grid_spec=pltpu.PrefetchScalarGridSpec(
            num_scalar_prefetch=1,
            grid=(blocks,),
            in_specs=[
                pl.BlockSpec((span, 4 * width), spot),
                pl.BlockSpec((1, width), fixed),
                pl.BlockSpec((1, width), fixed),
                pl.BlockSpec((1, 1, span), lambda step, info: (blocks - 1 - step, 0, 0)),
                pl.BlockSpec((span, width), spot),
                pl.BlockSpec((span, width), spot),
                pl.BlockSpec(
                    (1, 2 * half_heads, HEAD_DIM, HEAD_DIM),
                    lambda step, info: (blocks - 1 - step, 0, 0, 0),
                ),
                pl.BlockSpec(
                    (1, 2 * half_heads, span, span), lambda step, info: (blocks - 1 - step, 0, 0, 0)
                ),
            ],
            out_specs=[
                pl.BlockSpec((span, 4 * width), spot),
                pl.BlockSpec((1, width), fixed),
                pl.BlockSpec((1, width), fixed),
            ],
            scratch_shapes=[pltpu.VMEM((2 * half_heads, HEAD_DIM, HEAD_DIM), f32)],
        ),
        compiler_params=pltpu.CompilerParams(vmem_limit_bytes=20 * 2**20),
        cost_estimate=pl.CostEstimate(
            flops=0, bytes_accessed=0, transcendentals=0
        ),
    )(info, proj, floor_row, gain_row, seg, mixed, grad, states, scores)


def stack_kernel(count, own, other, *refs):
    outs, sems = refs[:count], refs[count]
    half = own.shape[1]
    copies = []
    for at in range(count):
        for side, source in enumerate((own, other)):
            target = outs[at].at[pl.ds(side * half, half)]
            copies.append(pltpu.make_async_copy(source.at[at], target, sems.at[at, side]))
    for copy in copies:
        copy.start()
    for copy in copies:
        copy.wait()


def stack_rows(own, other, room=4):
    count, rows, depth = own.shape
    return pl.pallas_call(
        functools.partial(stack_kernel, count),
        out_shape=[jax.ShapeDtypeStruct((2 * rows, depth), own.dtype)] * count,
        in_specs=[pl.BlockSpec(memory_space=pl.ANY)] * 2,
        out_specs=[pl.BlockSpec(memory_space=pltpu.VMEM)] * count,
        scratch_shapes=[pltpu.SemaphoreType.DMA((count, 2))],
        compiler_params=pltpu.CompilerParams(vmem_limit_bytes=room * 2**20),
        cost_estimate=pl.CostEstimate(flops=0, bytes_accessed=0, transcendentals=0),
    )(own, other)


def free_call(kernel, out_shape, megabytes, *args):
    vmem = pl.BlockSpec(memory_space=pltpu.VMEM)
    return pl.pallas_call(
        kernel,
        out_shape=out_shape,
        in_specs=[vmem] * len(args),
        out_specs=jax.tree.map(lambda _: vmem, out_shape),
        compiler_params=pltpu.CompilerParams(vmem_limit_bytes=megabytes * 2**20),
        cost_estimate=pl.CostEstimate(flops=0, bytes_accessed=0, transcendentals=0),
    )(*args)


def add_kernel(left, right, *refs):
    out = refs[-1]
    out[0] = (left[...].astype(f32) + right[...].astype(f32)).astype(bf16)


def add_pair(left, right, count=1, at=0, before=None):
    rows, depth = left.shape
    step = rows
    while step > 256 and step % 32 == 0:
        step //= 2
    block = pl.BlockSpec((step, depth), lambda index: (index, 0))
    return pl.pallas_call(
        add_kernel,
        out_shape=jax.ShapeDtypeStruct((count, rows, depth), bf16),
        grid=(rows // step,),
        in_specs=[block] * 2 + ([] if before is None else [pl.BlockSpec(memory_space=pl.ANY)]),
        out_specs=pl.BlockSpec((1, step, depth), lambda index: (at, index, 0)),
        input_output_aliases={} if before is None else {2: 0},
        compiler_params=pltpu.CompilerParams(vmem_limit_bytes=10 * 2**20),
        cost_estimate=pl.CostEstimate(flops=0, bytes_accessed=0, transcendentals=0),
    )(*((left, right) if before is None else (left, right, before)))


def pieces(lefts, rights):
    found, left, right, start, begin = [], 0, 0, 0, 0
    while left < len(lefts):
        rows = min(lefts[left].shape[0] - start, rights[right].shape[0] - begin)
        found.append(((lefts[left], start), (rights[right], begin), rows))
        start, begin = start + rows, begin + rows
        if start == lefts[left].shape[0]:
            left, start = left + 1, 0
        if begin == rights[right].shape[0]:
            right, begin = right + 1, 0
    return found


def cross_kernel(count, by_rows, *refs):
    own, other = refs[-2:]
    rows = refs[0].shape[1]
    width = refs[count].shape[1]
    step = 512 if rows < 2048 else 256
    step = step if (width if by_rows else width // 2) % step == 0 else width // 2
    found = pieces(refs[:count], refs[count:-2])
    for col in range(0, width, step):
        lanes = slice(col, col + step)
        total, lefts, rights, held = None, [], [], 0
        for index, ((one, start), (two, begin), tokens) in enumerate(found):
            lefts.append(one[start : start + tokens])
            rights.append(two[begin : begin + tokens, lanes])
            held += tokens
            if held >= 256 or index == len(found) - 1:
                left = lefts[0] if len(lefts) == 1 else jnp.concatenate(lefts)
                right = rights[0] if len(rights) == 1 else jnp.concatenate(rights)
                term = mm(left, right, TN)
                total = term if total is None else total + term
                lefts, rights, held = [], [], 0
        if by_rows:
            own[:, lanes] = total[: rows // 2].astype(bf16)
            other[:, lanes] = total[rows // 2 :].astype(bf16)
        elif col < width // 2:
            own[:, lanes] = total.astype(bf16)
        else:
            other[:, col - width // 2 : col - width // 2 + step] = total.astype(bf16)


def cross(lefts, rights, by_rows=True):
    rows, width = lefts[0].shape[1], rights[0].shape[1]
    half = (rows // 2, width) if by_rows else (rows, width // 2)
    out = [jax.ShapeDtypeStruct(half, bf16)] * 2
    return free_call(functools.partial(cross_kernel, len(lefts), by_rows), out, 10, *lefts, *rights)


def per_device(
    size,
    depth,
    layer_input,
    doc_starts,
    norm1_gain,
    w_query,
    w_forget,
    w_input,
    w_gate_out,
    forget_floor,
    group_gain,
    w_out,
    norm2_gain,
    ffn_gate,
    ffn_up,
    ffn_down,
    out_cotangent,
):
    row_count, shard_len, model_width = layer_input.shape
    assert row_count == 2 and size & (size - 1) == 0
    seq_len = doc_starts.shape[1]
    half_width = w_query.shape[1]
    half_heads = half_width // HEAD_DIM
    width = 2 * half_width
    me = lax.axis_index("head")
    place = lax.axis_index("dp")
    row = me % 2
    bits = [1 << at for at in range(1, size.bit_length() - 1)]
    own_tokens = 2 * shard_len
    hidden_dev = ffn_gate.shape[1]
    hidden_half = depth * hidden_dev

    def pick(tensor, at):
        return lax.dynamic_index_in_dim(tensor, at, 0, keepdims=False)

    def to_row(tensor):
        return jnp.concatenate((pick(tensor, row), swap(pick(tensor, 1 - row), 1, size)))

    def from_row(tensor):
        mine, other = tensor[:shard_len], swap(tensor[shard_len:], 1, size)
        return jnp.where(row == 0, jnp.stack((mine, other)), jnp.stack((other, mine)))

    two = len(bits) == 2

    def chunk(tensor, at):
        return tensor[at * own_tokens : (at + 1) * own_tokens]

    pair_rows = layer_input.astype(f32)
    pair_scale = rms_scale(pair_rows)
    pair_normed = (pair_rows * pair_scale * norm1_gain).astype(bf16)
    normed_mine, normed_theirs = pick(pair_normed, row), pick(pair_normed, 1 - row)
    normed_sib = swap(normed_theirs, 1, size)
    if two:
        first, second = bits
        near_first = [swap(normed_mine, first, size), swap(normed_theirs, first | 1, size)]
        near_second = [swap(normed_mine, second, size), swap(normed_theirs, second | 1, size)]
        far = [swap(near_first[0], second, size), swap(near_second[1], first, size)]
        normed_parts = [normed_mine, normed_sib, *near_first, *near_second, *far]
    else:
        normed_parts = gather_start(jnp.concatenate((normed_mine, normed_sib)), bits, size)[1]

    normed_parts[1], out_cotangent = tie(normed_parts[1], out_cotangent)
    cot_own = to_row(out_cotangent)

    gate_up = lax.all_gather(jnp.stack((ffn_gate.T, ffn_up.T)), "dp", axis=1, tiled=True)
    down = lax.all_gather(ffn_down.T, "dp", axis=0, tiled=True)

    proj_own = jnp.concatenate((w_query, w_forget, w_input, w_gate_out), axis=1)
    proj_weights = jnp.concatenate((proj_own, swap(proj_own, 1, size)), axis=1)
    vectors = jnp.stack((forget_floor, group_gain))
    vectors = jnp.concatenate((vectors, swap(vectors, 1, size)), axis=1)
    floor_row, gain_row = vectors[:1], vectors[1:]

    seg = jnp.cumsum(pick(doc_starts, row)).reshape(size, shard_len)
    seg_last = seg[:, -1]
    info = jnp.concatenate((me[None], jnp.zeros((1,), jnp.int32), seg_last[:-1], seg_last))
    seg = seg[:, None, :]

    proj = jnp.zeros((seq_len, 4 * width), f32)
    at = 0
    early = len(normed_parts) * 3 // 4 if two else 0
    for index, part in enumerate(normed_parts):
        if two and index == early:
            proj, *normed_parts[early:], cot_own, layer_input, w_out = tie(
                proj, *normed_parts[early:], cot_own, layer_input, w_out
            )
            part = normed_parts[index]
        if two and index >= early:
            if index == early:
                continue
            part = jnp.concatenate(normed_parts[early:])
        proj = lax.dynamic_update_slice(proj, mm(part, proj_weights, NN), (at, 0))
        at += part.shape[0]
    gated, mixed, states, scores = recurrence(
        info, proj, floor_row, gain_row, seg, half_heads, size
    )
    out_weights = jnp.concatenate((w_out, swap(w_out, 1, size)))

    own_rows = to_row(layer_input)
    if two:
        cot_near = gather_near(cot_own, bits, size)
        gated, cot_near, own_rows = tie(gated, cot_near, own_rows)
    own_rows = own_rows.astype(f32)

    mixer_sum = Scatter(lambda at: mm(chunk(gated, at), out_weights, NN).astype(bf16), bits, size)
    resid = own_rows + mixer_sum.total(own_rows)[0]
    row_scale = rms_scale(resid)
    ffn_own = (resid * row_scale * norm2_gain).astype(bf16)
    ffn_own, gate_up = tie(ffn_own, gate_up)
    if two:
        ffn_near = gather_near(ffn_own, bits, size)
        ffn_near, cot_near = tie(ffn_near, cot_near)
        ffn_far = gather_far(ffn_near, bits, size)
        cot_flat = [cot_own, *cot_near, *gather_far(cot_near, bits, size)]
        ffn_parts = [ffn_own, *ffn_near, ffn_far]
    else:
        ffn_parts = gather_start(ffn_own, bits, size)[1]
        cot_flat = gather_start(cot_own, bits, size)[1]
    ffn_flat = [*ffn_parts[:3], *ffn_parts[3]] if two else ffn_parts
    count = len(ffn_parts)
    gate_rows, up_rows = stack_rows(gate_up, swap(gate_up, 1, size))

    gate_part, up_part, inner = [], [], []
    for at in range(count):
        if at:
            ffn_parts[at], inner[-1] = tie(ffn_parts[at], inner[-1])
        if at == count - 1:
            ffn_parts[at], cot_flat = tie(ffn_parts[at], cot_flat)
        if two and at == 3:
            ffn_parts[3] = jnp.concatenate(ffn_parts[3])
        gate, up = mm(ffn_parts[at], gate_rows, NT), mm(ffn_parts[at], up_rows, NT)
        sig = jax.nn.sigmoid(gate)
        silu = gate * sig
        kept = tie(
            silu.astype(bf16),
            (up * sig * (1.0 + gate * (1.0 - sig))).astype(bf16),
            (silu * up).astype(bf16),
        )
        for held, one in zip((up_part, gate_part, inner), kept):
            held.append(one)
    inner[-1], down = tie(inner[-1], down)
    down_own, down_other = cross(inner, cot_flat)
    down_received, down_own = tie(swap(down, 1, size), down_own)
    down_other = swap(down_other, 1, size)
    down_pair = None
    (down_rows,) = stack_rows(down[None], down_received[None])
    cot_parts = [*cot_flat[:3], jnp.concatenate(cot_flat[3:])] if two else cot_flat
    gate_grad, up_grad, totals = [None] * count, [None] * count, []

    def ffn_part(at):
        nonlocal down_other, down_pair
        part = cot_parts[at]
        if len(totals) == 1:
            down_other, totals[0] = tie(down_other, totals[0])
            down_pair = add_pair(down_own, down_other)[0]
            part, down_pair = tie(part, down_pair)
        if totals:
            part, totals[-1] = tie(part, totals[-1])
        inner_grad = mm(part, down_rows, NT)
        gate_grad[at] = (inner_grad * gate_part[at].astype(f32)).astype(bf16)
        up_grad[at] = (inner_grad * up_part[at].astype(f32)).astype(bf16)
        totals.append(
            add(mm(gate_grad[at], gate_rows, NN), mm(up_grad[at], up_rows, NN)).astype(bf16)
        )
        return totals[-1]

    ffn_sum = Scatter(ffn_part, bits, size)
    ffn_down_grad = lax.psum_scatter(down_pair, "dp", scatter_dimension=0, tiled=True)
    if two:
        ffn_sum.own, gate_grad[0] = tie(ffn_sum.own, gate_grad[0])
    gate_own, gate_other = cross(gate_grad, ffn_flat)
    gate_other, up_grad[0] = tie(gate_other, up_grad[0])
    up_own, up_other = cross(up_grad, ffn_flat)
    up_other, ffn_down_grad = tie(up_other, ffn_down_grad)
    if two:
        ffn_sum.moved, up_other = tie(ffn_sum.moved, up_other)
        ffn_sum.finish()
    gate_up_pair = add_pair(gate_own, swap(gate_other, 1, size), 2, 0)
    gate_up_pair, up_own = tie(gate_up_pair, up_own)
    gate_up_pair = add_pair(up_own, swap(up_other, 1, size), 2, 1, gate_up_pair)
    ffn_in_grad = ffn_sum.total(resid)[0]
    gate_up_grad = lax.psum_scatter(gate_up_pair, "dp", scatter_dimension=1, tiled=True)

    scaled = ffn_in_grad * norm2_gain
    resid_grad = cot_own.astype(f32) + row_scale * (
        scaled - resid * row_scale * row_scale * jnp.mean(scaled * resid, axis=-1, keepdims=True)
    )
    norm2_part = jnp.sum(ffn_in_grad * resid * row_scale, axis=0)
    mixer_parts = gather_start(resid_grad.astype(bf16), bits, size)[1]
    output_parts = [mm(inner[at], down_rows, NN).astype(bf16) for at in range(count)]
    output_parts, mixer_parts[-1] = tie(output_parts, mixer_parts[-1])
    output_sum = Scatter(lambda at: output_parts[at], bits, size)
    mixer_grad = jnp.concatenate(mixer_parts)

    out_own, out_other = cross([gated], mixer_parts)
    mixer_grad, out_other = tie(mixer_grad, out_other)
    out_pair = add_pair(out_own, swap(out_other, 1, size))[0]
    gated_grad = mm(mixer_grad, out_weights, NT)
    proj_grad, floor_grad, gain_grad = recurrence_back(
        info, proj, floor_row, gain_row, seg, mixed, gated_grad, states, scores, half_heads, size
    )
    if two:
        output_sum.moved, proj_grad = tie(output_sum.moved, proj_grad)

    proj_grad, out_pair = tie(proj_grad, out_pair)
    proj_own, proj_other = cross(normed_parts, [proj_grad], by_rows=False)
    proj_other, proj_grad, gate_up_grad = tie(proj_other, proj_grad, gate_up_grad)
    normed_all = mm(proj_grad, proj_weights, NT).astype(bf16)
    proj_other, normed_all, floor_grad = tie(swap(proj_other, 1, size), normed_all, floor_grad)
    proj_pair = add_pair(proj_own, proj_other)[0]
    normed_sum = Scatter(lambda at: chunk(normed_all, at), bits, size)
    if two:
        normed_sum.finish()
    normed_grad = normed_sum.total(proj_own)[0]
    out_grad = lax.psum_scatter(out_pair, "dp", scatter_dimension=1, tiled=True)
    proj_pair, out_grad = tie(proj_pair, out_grad)
    proj_w_grad = lax.psum_scatter(proj_pair, "dp", scatter_dimension=0, tiled=True).astype(f32)

    input_scale = rms_scale(own_rows)
    scaled_in = normed_grad * norm1_gain
    input_grad = resid_grad + input_scale * (
        scaled_in
        - own_rows
        * input_scale
        * input_scale
        * jnp.mean(scaled_in * own_rows, axis=-1, keepdims=True)
    )
    norm1_part = jnp.sum(normed_grad * own_rows * input_scale, axis=0)
    input_grad = from_row(input_grad)

    if two:
        output_sum.finish()
        output_sum.sends, norm1_part = tie(output_sum.sends, norm1_part)
    output = from_row(add(resid, output_sum.total(resid)[0]).astype(bf16))

    vector_grads = jnp.concatenate((gain_grad, floor_grad))
    vector_grads = vector_grads[:, :half_width] + swap(vector_grads[:, half_width:], 1, size)
    moved = [
        lax.ppermute(vector_grads, "dp", [(at, (at + slot) % depth) for at in range(depth)])
        for slot in range(1, depth)
    ]
    vector_grads = sum(moved, vector_grads)
    vector_len = half_width // depth
    vector_grads = lax.dynamic_slice_in_dim(vector_grads, place * vector_len, vector_len, 1)
    norm_grads = jnp.stack((norm1_part, norm2_part))
    for bit in [1] + bits:
        norm_grads = norm_grads + swap(norm_grads, bit, size)
    moved = [
        lax.ppermute(norm_grads, "dp", [(at, (at + slot) % depth) for at in range(depth)])
        for slot in range(1, depth)
    ]
    stacked = jnp.stack([norm_grads] + moved)
    order = (place - jnp.arange(depth)) % depth
    norm_grads = jnp.sum(jnp.zeros_like(stacked).at[order].set(stacked), axis=0)

    return (
        output,
        input_grad,
        proj_w_grad[:, 0:half_width],
        proj_w_grad[:, half_width : 2 * half_width],
        proj_w_grad[:, 2 * half_width : 3 * half_width],
        proj_w_grad[:, 3 * half_width : 4 * half_width],
        out_grad.astype(f32),
        vector_grads[0],
        vector_grads[1],
        norm_grads[0],
        norm_grads[1],
        gate_up_grad[0].astype(f32).T,
        gate_up_grad[1].astype(f32).T,
        ffn_down_grad.astype(f32).T,
    )


def solution(mesh):
    placed = (
        P("dp", "head", None),
        P("dp", None),
        P(),
        P(None, "head"),
        P(None, "head"),
        P(None, "head"),
        P(None, "head"),
        P("head"),
        P("head"),
        P("head", None),
        P(),
        P(None, ("head", "dp")),
        P(None, ("head", "dp")),
        P(None, ("head", "dp")),
        P("dp", "head", None),
    )
    return jax.shard_map(
        functools.partial(per_device, mesh.shape["head"], mesh.shape["dp"]),
        mesh=mesh,
        in_specs=placed,
        out_specs=(
            P("dp", "head", None),
            P("dp", "head", None),
            P("dp", "head"),
            P("dp", "head"),
            P("dp", "head"),
            P("dp", "head"),
            P("head", "dp"),
            P(("head", "dp")),
            P(("head", "dp")),
            P(),
            P(),
            P(None, ("head", "dp")),
            P(None, ("head", "dp")),
            P(None, ("head", "dp")),
        ),
        check_vma=False,
    )
```

```python
import functools

import jax
import jax.numpy as jnp
from jax import lax
from jax.experimental import pallas as pl
from jax.experimental.pallas import tpu as pltpu
from jax.sharding import PartitionSpec as P

HEAD_DIM = 128
epsilon = 1e-06
f32 = jnp.float32
bf16 = jnp.bfloat16


def swap(tensor, bit, size):
    return lax.ppermute(tensor, "head", [(at, at ^ bit) for at in range(size)])


def mm(left, right, dims, out=f32):
    return lax.dot_general(left, right, (dims, ((), ())), preferred_element_type=out)


NN = ((1,), (0,))
NT = ((1,), (1,))
TN = ((0,), (0,))


def rms_scale(tensor):
    return lax.rsqrt(jnp.mean(tensor * tensor, axis=-1, keepdims=True) + epsilon)


def gather_near(own, bits, size):
    return swap(own, bits[0], size), swap(own, bits[1], size)


def gather_far(near, bits, size):
    half = near[0].shape[0] // 2
    return swap(near[0][:half], bits[1], size), swap(near[1][half:], bits[0], size)


def gather_start(own, bits, size):
    if len(bits) == 2:
        near = gather_near(own, bits, size)
        return near, [own, *near, *gather_far(near, bits, size)]
    parts = [own]
    for bit in bits:
        moved = swap(jnp.stack(parts), bit, size)
        parts = parts + [moved[at] for at in range(len(parts))]
    return parts[1:], parts


class Scatter:
    def __init__(self, part_of, bits, size):
        self.bits, self.size = bits, size
        self.moved, self.sends = [], None
        if len(bits) == 2:
            first, second = bits
            both = part_of(3)
            self.half = half = both.shape[0] // 2
            top_both, bottom_both = swap(both[:half], first, size), swap(both[half:], second, size)
            self.at_first, self.at_second = part_of(1), part_of(2)
            top_first = swap(self.at_first[:half], first, size)
            bottom_second = swap(self.at_second[half:], second, size)
            self.moved = [top_both, bottom_both, top_first, bottom_second]
            self.own = part_of(0)
        else:
            self.parts = [part_of(at) for at in range(1 << len(bits))]

    def finish(self):
        self.moved = list(tie(*self.moved))
        top_both, bottom_both = self.moved[:2]
        self.sends = (
            add(self.at_first[self.half :], bottom_both).astype(bf16),
            add(self.at_second[: self.half], top_both).astype(bf16),
        )

    def total(self, held=None):
        bits, size = self.bits, self.size
        if len(bits) == 2:
            first, second = bits
            if self.sends is None:
                self.finish()
            bottom_first, top_second = swap(self.sends[0], first, size), swap(self.sends[1], second, size)
            bottom_first, top_second, held = tie(bottom_first, top_second, held)
            top_first, bottom_second = self.moved[2:]
            top = add(self.own[: self.half], top_first, top_second)
            bottom = add(self.own[self.half :], bottom_first, bottom_second)
            return jnp.concatenate((top, bottom)), held
        parts = [part.astype(f32) for part in self.parts]
        for bit in reversed(bits):
            count = len(parts) // 2
            moved = swap(jnp.stack(parts[count:]).astype(bf16), bit, size)
            parts = [add(parts[at], moved[at]) for at in range(count)]
        return parts[0], held


def add(first, *rest):
    total = first.astype(f32)
    for term in rest:
        total = total + term.astype(f32)
    return total


def tie(*tensors):
    return lax.optimization_barrier(tensors)


def halves(tensor):
    high = tensor.astype(bf16)
    return high, (tensor - high.astype(f32)).astype(bf16)


def cumulate(triangle, tensor):
    high, low = halves(tensor)
    return mm(triangle, high, NN) + mm(triangle, low, NN)


def span_masks(info, block, blocks, seg_ref):
    span = seg_ref.shape[-1]
    across = jnp.broadcast_to(seg_ref[0], (span, span))
    down = across.T
    rows = lax.broadcasted_iota(jnp.int32, (span, span), 0)
    cols = lax.broadcasted_iota(jnp.int32, (span, span), 1)
    before = info[1 + block]
    last = info[1 + blocks + block]
    same = (across == down) & (rows >= cols)
    column = down[:, :1]
    carried = (column == before).astype(f32)
    to_final = (column == last).astype(f32)
    through = (before == last).astype(f32)
    return rows, cols, same, carried, to_final, through


def head_columns(head, half_heads, half_width):
    base = (head // half_heads) * 4 * half_width + (head % half_heads) * HEAD_DIM
    return [slice(base + at * half_width, base + at * half_width + HEAD_DIM) for at in range(4)]


def forward_kernel(
    blocks, half_heads, info, proj_ref, floor_ref, gain_ref, seg_ref, gated_ref, mixed_ref, states_ref, scores_ref, state
):
    block = pl.program_id(0)
    half_width = half_heads * HEAD_DIM

    @pl.when(block == 0)
    def _():
        state[...] = jnp.zeros_like(state)

    rows, cols, same, carried, to_final, through = span_masks(info, block, blocks, seg_ref)
    span = rows.shape[0]
    lower = (rows >= cols).astype(bf16)
    for head in range(2 * half_heads):
        lanes = slice(head * HEAD_DIM, (head + 1) * HEAD_DIM)
        at_q, at_f, at_v, at_g = head_columns(head, half_heads, half_width)
        queries, forget_pre = proj_ref[:, at_q], proj_ref[:, at_f]
        values, gate = proj_ref[:, at_v].astype(bf16), proj_ref[:, at_g]
        inject = (1.0 - floor_ref[:, lanes]) / (1.0 + jnp.exp(forget_pre))
        decays = cumulate(lower, jnp.log(1.0 - inject))
        last = decays[span - 1 :, :]
        lifted, lifted_rest = halves(queries * jnp.exp(decays))
        lowered, lowered_rest = halves(inject * jnp.exp(-decays))
        scores = mm(lifted, lowered, NT) + mm(lifted, lowered_rest, NT) + mm(lifted_rest, lowered, NT)
        scores = jnp.where(same, scores, 0.0).astype(bf16)
        scores_ref[0, head] = scores
        now = state[head]
        states_ref[0, head] = now
        mixed = mm(scores, values, NN) + carried * mm(lifted, now.astype(bf16), NT)
        kept = (inject * jnp.exp(last - decays) * to_final).astype(bf16)
        state[head] = now * (jnp.exp(last) * through) + mm(values, kept, TN)
        mixed_ref[:, lanes] = mixed
        grouped = mixed * rms_scale(mixed) * gain_ref[:, lanes]
        gated_ref[:, lanes] = (grouped * gate / (1.0 + jnp.exp(-gate))).astype(bf16)


def backward_kernel(
    blocks, half_heads, info, proj_ref, floor_ref, gain_ref, seg_ref, mixed_ref, grad_ref, states_ref, scores_ref,
    proj_grad_ref, floor_grad_ref, gain_grad_ref, state_grad,
):
    step = pl.program_id(0)
    block = blocks - 1 - step
    half_width = half_heads * HEAD_DIM

    @pl.when(step == 0)
    def _():
        state_grad[...] = jnp.zeros_like(state_grad)
        floor_grad_ref[...] = jnp.zeros_like(floor_grad_ref)
        gain_grad_ref[...] = jnp.zeros_like(gain_grad_ref)

    rows, cols, same, carried, to_final, through = span_masks(info, block, blocks, seg_ref)
    span = rows.shape[0]
    lower = (rows >= cols).astype(bf16)
    upper = (rows <= cols).astype(bf16)
    is_last = lax.broadcasted_iota(jnp.int32, (span, 1), 0) == span - 1
    for head in range(2 * half_heads):
        lanes = slice(head * HEAD_DIM, (head + 1) * HEAD_DIM)
        at_q, at_f, at_v, at_g = head_columns(head, half_heads, half_width)
        queries, forget_pre = proj_ref[:, at_q], proj_ref[:, at_f]
        values, gate = proj_ref[:, at_v].astype(bf16), proj_ref[:, at_g]
        mixed, gain, grad = mixed_ref[:, lanes], gain_ref[:, lanes], grad_ref[:, lanes]
        gate_sig = 1.0 / (1.0 + jnp.exp(-gate))
        scale = rms_scale(mixed)
        unit = mixed * scale
        grouped_grad = grad * gate * gate_sig
        proj_grad_ref[:, at_g] = (
            grad * unit * gain * gate_sig * (1.0 + gate * (1.0 - gate_sig))
        ).astype(bf16)
        gain_grad_ref[:, lanes] += jnp.sum(grouped_grad * unit, axis=0, keepdims=True)
        unit_grad = grouped_grad * gain
        mixed_grad, mixed_rest = halves(
            scale * (unit_grad - unit * jnp.mean(unit_grad * unit, axis=-1, keepdims=True))
        )
        room = 1.0 - floor_ref[:, lanes]
        sig = 1.0 / (1.0 + jnp.exp(forget_pre))
        inject = room * sig
        decays = cumulate(lower, jnp.log(1.0 - inject))
        last = decays[span - 1 :, :]
        rise, fall, rest = jnp.exp(decays), jnp.exp(-decays), jnp.exp(last - decays) * to_final
        lifted = (queries * rise).astype(bf16)
        lowered = (inject * fall).astype(bf16)
        kept = (inject * rest).astype(bf16)
        scores = scores_ref[0, head]
        scores_grad = mm(mixed_grad, values, NT) + mm(mixed_rest, values, NT)
        scores_grad = jnp.where(same, scores_grad, 0.0).astype(bf16)
        now, after = states_ref[0, head], state_grad[head]
        after_low, now_low = after.astype(bf16), now.astype(bf16)
        state_part = mm(mixed_grad, now_low, NN) + mm(mixed_rest, now_low, NN)
        lifted_grad = mm(scores_grad, lowered, NN) + carried * state_part
        lowered_grad = mm(scores_grad, lifted, TN)
        kept_grad = mm(values, after_low, NN)
        value_grad = mm(scores, mixed_grad, TN) + mm(kept, after_low, NT)
        kept_term = kept_grad * kept.astype(f32)
        decay_grad = lifted_grad * lifted.astype(f32) - lowered_grad * lowered.astype(f32) - kept_term
        pass_on = jnp.exp(last) * through
        last_grad = jnp.sum(kept_term, axis=0, keepdims=True) + pass_on * jnp.sum(
            now * after, axis=0, keepdims=True
        )
        decay_grad = decay_grad + jnp.where(is_last, last_grad, 0.0)
        log_grad = cumulate(upper, decay_grad)
        inject_grad = lowered_grad * fall + kept_grad * rest - log_grad / (1.0 - inject)
        state_grad[head] = after * pass_on + mm(
            mixed_grad, (lifted.astype(f32) * carried).astype(bf16), TN
        )
        proj_grad_ref[:, at_q] = (lifted_grad * rise).astype(bf16)
        proj_grad_ref[:, at_f] = (-inject_grad * room * sig * (1.0 - sig)).astype(bf16)
        proj_grad_ref[:, at_v] = value_grad.astype(bf16)
        floor_grad_ref[:, lanes] -= jnp.sum(inject_grad * sig, axis=0, keepdims=True)


def recurrence(info, proj, floor_row, gain_row, seg, half_heads, size):
    blocks, _, span = seg.shape
    width = floor_row.shape[1]
    spot = lambda block, info: (block ^ info[0], 0)
    fixed = lambda block, info: (0, 0)
    return pl.pallas_call(
        functools.partial(forward_kernel, blocks, half_heads),
        out_shape=(
            jax.ShapeDtypeStruct((blocks * span, width), bf16),
            jax.ShapeDtypeStruct((blocks * span, width), f32),
            jax.ShapeDtypeStruct((blocks, 2 * half_heads, HEAD_DIM, HEAD_DIM), f32),
            jax.ShapeDtypeStruct((blocks, 2 * half_heads, span, span), bf16),
        ),
        grid_spec=pltpu.PrefetchScalarGridSpec(
            num_scalar_prefetch=1,
            grid=(blocks,),
            in_specs=[
                pl.BlockSpec((span, 4 * width), spot),
                pl.BlockSpec((1, width), fixed),
                pl.BlockSpec((1, width), fixed),
                pl.BlockSpec((1, 1, span), lambda block, info: (block, 0, 0)),
            ],
            out_specs=[
                pl.BlockSpec((span, width), spot),
                pl.BlockSpec((span, width), spot),
                pl.BlockSpec(
                    (1, 2 * half_heads, HEAD_DIM, HEAD_DIM), lambda block, info: (block, 0, 0, 0)
                ),
                pl.BlockSpec((1, 2 * half_heads, span, span), lambda block, info: (block, 0, 0, 0)),
            ],
            scratch_shapes=[pltpu.VMEM((2 * half_heads, HEAD_DIM, HEAD_DIM), f32)],
        ),
        compiler_params=pltpu.CompilerParams(vmem_limit_bytes=16 * 2**20),
        cost_estimate=pl.CostEstimate(
            flops=0, bytes_accessed=0, transcendentals=0
        ),
    )(info, proj, floor_row, gain_row, seg)


def recurrence_back(info, proj, floor_row, gain_row, seg, mixed, grad, states, scores, half_heads, size):
    blocks, _, span = seg.shape
    width = floor_row.shape[1]
    spot = lambda step, info: ((blocks - 1 - step) ^ info[0], 0)
    fixed = lambda step, info: (0, 0)
    return pl.pallas_call(
        functools.partial(backward_kernel, blocks, half_heads),
        out_shape=(
            jax.ShapeDtypeStruct((blocks * span, 4 * width), bf16),
            jax.ShapeDtypeStruct((1, width), f32),
            jax.ShapeDtypeStruct((1, width), f32),
        ),
        grid_spec=pltpu.PrefetchScalarGridSpec(
            num_scalar_prefetch=1,
            grid=(blocks,),
            in_specs=[
                pl.BlockSpec((span, 4 * width), spot),
                pl.BlockSpec((1, width), fixed),
                pl.BlockSpec((1, width), fixed),
                pl.BlockSpec((1, 1, span), lambda step, info: (blocks - 1 - step, 0, 0)),
                pl.BlockSpec((span, width), spot),
                pl.BlockSpec((span, width), spot),
                pl.BlockSpec(
                    (1, 2 * half_heads, HEAD_DIM, HEAD_DIM),
                    lambda step, info: (blocks - 1 - step, 0, 0, 0),
                ),
                pl.BlockSpec(
                    (1, 2 * half_heads, span, span), lambda step, info: (blocks - 1 - step, 0, 0, 0)
                ),
            ],
            out_specs=[
                pl.BlockSpec((span, 4 * width), spot),
                pl.BlockSpec((1, width), fixed),
                pl.BlockSpec((1, width), fixed),
            ],
            scratch_shapes=[pltpu.VMEM((2 * half_heads, HEAD_DIM, HEAD_DIM), f32)],
        ),
        compiler_params=pltpu.CompilerParams(vmem_limit_bytes=20 * 2**20),
        cost_estimate=pl.CostEstimate(
            flops=0, bytes_accessed=0, transcendentals=0
        ),
    )(info, proj, floor_row, gain_row, seg, mixed, grad, states, scores)


def stack_kernel(count, own, other, *refs):
    outs, sems = refs[:count], refs[count]
    half = own.shape[1]
    copies = []
    for at in range(count):
        for side, source in enumerate((own, other)):
            target = outs[at].at[pl.ds(side * half, half)]
            copies.append(pltpu.make_async_copy(source.at[at], target, sems.at[at, side]))
    for copy in copies:
        copy.start()
    for copy in copies:
        copy.wait()


def stack_rows(own, other, room=4):
    count, rows, depth = own.shape
    return pl.pallas_call(
        functools.partial(stack_kernel, count),
        out_shape=[jax.ShapeDtypeStruct((2 * rows, depth), own.dtype)] * count,
        in_specs=[pl.BlockSpec(memory_space=pl.ANY)] * 2,
        out_specs=[pl.BlockSpec(memory_space=pltpu.VMEM)] * count,
        scratch_shapes=[pltpu.SemaphoreType.DMA((count, 2))],
        compiler_params=pltpu.CompilerParams(vmem_limit_bytes=room * 2**20),
        cost_estimate=pl.CostEstimate(flops=0, bytes_accessed=0, transcendentals=0),
    )(own, other)


def free_call(kernel, out_shape, megabytes, *args):
    vmem = pl.BlockSpec(memory_space=pltpu.VMEM)
    return pl.pallas_call(
        kernel,
        out_shape=out_shape,
        in_specs=[vmem] * len(args),
        out_specs=jax.tree.map(lambda _: vmem, out_shape),
        compiler_params=pltpu.CompilerParams(vmem_limit_bytes=megabytes * 2**20),
        cost_estimate=pl.CostEstimate(flops=0, bytes_accessed=0, transcendentals=0),
    )(*args)


def add_kernel(left, right, *refs):
    out = refs[-1]
    out[0] = (left[...].astype(f32) + right[...].astype(f32)).astype(bf16)


def add_pair(left, right, count=1, at=0, before=None):
    rows, depth = left.shape
    step = rows
    while step > 256 and step % 32 == 0:
        step //= 2
    block = pl.BlockSpec((step, depth), lambda index: (index, 0))
    return pl.pallas_call(
        add_kernel,
        out_shape=jax.ShapeDtypeStruct((count, rows, depth), bf16),
        grid=(rows // step,),
        in_specs=[block] * 2 + ([] if before is None else [pl.BlockSpec(memory_space=pl.ANY)]),
        out_specs=pl.BlockSpec((1, step, depth), lambda index: (at, index, 0)),
        input_output_aliases={} if before is None else {2: 0},
        compiler_params=pltpu.CompilerParams(vmem_limit_bytes=10 * 2**20),
        cost_estimate=pl.CostEstimate(flops=0, bytes_accessed=0, transcendentals=0),
    )(*((left, right) if before is None else (left, right, before)))


def pieces(lefts, rights):
    found, left, right, start, begin = [], 0, 0, 0, 0
    while left < len(lefts):
        rows = min(lefts[left].shape[0] - start, rights[right].shape[0] - begin)
        found.append(((lefts[left], start), (rights[right], begin), rows))
        start, begin = start + rows, begin + rows
        if start == lefts[left].shape[0]:
            left, start = left + 1, 0
        if begin == rights[right].shape[0]:
            right, begin = right + 1, 0
    return found


def cross_kernel(count, by_rows, *refs):
    own, other = refs[-2:]
    rows = refs[0].shape[1]
    width = refs[count].shape[1]
    step = 512 if rows < 2048 else 256
    step = step if (width if by_rows else width // 2) % step == 0 else width // 2
    found = pieces(refs[:count], refs[count:-2])
    for col in range(0, width, step):
        lanes = slice(col, col + step)
        total, lefts, rights, held = None, [], [], 0
        for index, ((one, start), (two, begin), tokens) in enumerate(found):
            lefts.append(one[start : start + tokens])
            rights.append(two[begin : begin + tokens, lanes])
            held += tokens
            if held >= 256 or index == len(found) - 1:
                left = lefts[0] if len(lefts) == 1 else jnp.concatenate(lefts)
                right = rights[0] if len(rights) == 1 else jnp.concatenate(rights)
                term = mm(left, right, TN)
                total = term if total is None else total + term
                lefts, rights, held = [], [], 0
        if by_rows:
            own[:, lanes] = total[: rows // 2].astype(bf16)
            other[:, lanes] = total[rows // 2 :].astype(bf16)
        elif col < width // 2:
            own[:, lanes] = total.astype(bf16)
        else:
            other[:, col - width // 2 : col - width // 2 + step] = total.astype(bf16)


def cross(lefts, rights, by_rows=True):
    rows, width = lefts[0].shape[1], rights[0].shape[1]
    half = (rows // 2, width) if by_rows else (rows, width // 2)
    out = [jax.ShapeDtypeStruct(half, bf16)] * 2
    return free_call(functools.partial(cross_kernel, len(lefts), by_rows), out, 10, *lefts, *rights)


def per_device(
    size,
    depth,
    layer_input,
    doc_starts,
    norm1_gain,
    w_query,
    w_forget,
    w_input,
    w_gate_out,
    forget_floor,
    group_gain,
    w_out,
    norm2_gain,
    ffn_gate,
    ffn_up,
    ffn_down,
    out_cotangent,
):
    row_count, shard_len, model_width = layer_input.shape
    assert row_count == 2 and size & (size - 1) == 0
    seq_len = doc_starts.shape[1]
    half_width = w_query.shape[1]
    half_heads = half_width // HEAD_DIM
    width = 2 * half_width
    me = lax.axis_index("head")
    place = lax.axis_index("dp")
    row = me % 2
    bits = [1 << at for at in range(1, size.bit_length() - 1)]
    own_tokens = 2 * shard_len
    hidden_dev = ffn_gate.shape[1]
    hidden_half = depth * hidden_dev

    def pick(tensor, at):
        return lax.dynamic_index_in_dim(tensor, at, 0, keepdims=False)

    def to_row(tensor):
        return jnp.concatenate((pick(tensor, row), swap(pick(tensor, 1 - row), 1, size)))

    def from_row(tensor):
        mine, other = tensor[:shard_len], swap(tensor[shard_len:], 1, size)
        return jnp.where(row == 0, jnp.stack((mine, other)), jnp.stack((other, mine)))

    two = len(bits) == 2

    def chunk(tensor, at):
        return tensor[at * own_tokens : (at + 1) * own_tokens]

    pair_rows = layer_input.astype(f32)
    pair_scale = rms_scale(pair_rows)
    pair_normed = (pair_rows * pair_scale * norm1_gain).astype(bf16)
    normed_mine, normed_theirs = pick(pair_normed, row), pick(pair_normed, 1 - row)
    normed_mine, normed_theirs, w_query = tie(normed_mine, normed_theirs, w_query)
    normed_sib = swap(normed_theirs, 1, size)
    if two:
        first, second = bits
        near_first = [swap(normed_mine, first, size), swap(normed_theirs, first | 1, size)]
        near_second = [swap(normed_mine, second, size), swap(normed_theirs, second | 1, size)]
        far = [swap(near_first[0], second, size), swap(near_second[1], first, size)]
        normed_parts = [normed_mine, normed_sib, *near_first, *near_second, *far]
    else:
        normed_parts = gather_start(jnp.concatenate((normed_mine, normed_sib)), bits, size)[1]

    normed_parts[1], out_cotangent = tie(normed_parts[1], out_cotangent)
    cot_own = to_row(out_cotangent)

    gate_up = lax.all_gather(jnp.stack((ffn_gate.T, ffn_up.T)), "dp", axis=1, tiled=True)
    down = lax.all_gather(ffn_down.T, "dp", axis=0, tiled=True)

    proj_own = jnp.concatenate((w_query, w_forget, w_input, w_gate_out), axis=1)
    proj_weights = jnp.concatenate((proj_own, swap(proj_own, 1, size)), axis=1)
    vectors = jnp.stack((forget_floor, group_gain))
    vectors = jnp.concatenate((vectors, swap(vectors, 1, size)), axis=1)
    floor_row, gain_row = vectors[:1], vectors[1:]

    seg = jnp.cumsum(pick(doc_starts, row)).reshape(size, shard_len)
    seg_last = seg[:, -1]
    info = jnp.concatenate((me[None], jnp.zeros((1,), jnp.int32), seg_last[:-1], seg_last))
    seg = seg[:, None, :]

    proj = jnp.zeros((seq_len, 4 * width), f32)
    at = 0
    early = len(normed_parts) * 3 // 4 if two else 0
    for index, part in enumerate(normed_parts):
        if two and index == early:
            proj, *normed_parts[early:], cot_own, layer_input, w_out = tie(
                proj, *normed_parts[early:], cot_own, layer_input, w_out
            )
            part = normed_parts[index]
        if two and index >= early:
            if index == early:
                continue
            part = jnp.concatenate(normed_parts[early:])
        proj = lax.dynamic_update_slice(proj, mm(part, proj_weights, NN), (at, 0))
        at += part.shape[0]
    gated, mixed, states, scores = recurrence(
        info, proj, floor_row, gain_row, seg, half_heads, size
    )
    out_weights = jnp.concatenate((w_out, swap(w_out, 1, size)))

    own_rows = to_row(layer_input)
    if two:
        cot_near = gather_near(cot_own, bits, size)
        gated, cot_near, own_rows = tie(gated, cot_near, own_rows)
    own_rows = own_rows.astype(f32)

    mixer_sum = Scatter(lambda at: mm(chunk(gated, at), out_weights, NN).astype(bf16), bits, size)
    resid = own_rows + mixer_sum.total(own_rows)[0]
    row_scale = rms_scale(resid)
    ffn_own = (resid * row_scale * norm2_gain).astype(bf16)
    ffn_own, gate_up = tie(ffn_own, gate_up)
    if two:
        ffn_near = gather_near(ffn_own, bits, size)
        ffn_near, cot_near = tie(ffn_near, cot_near)
        ffn_far = gather_far(ffn_near, bits, size)
        cot_flat = [cot_own, *cot_near, *gather_far(cot_near, bits, size)]
        ffn_parts = [ffn_own, *ffn_near, ffn_far]
    else:
        ffn_parts = gather_start(ffn_own, bits, size)[1]
        cot_flat = gather_start(cot_own, bits, size)[1]
    ffn_flat = [*ffn_parts[:3], *ffn_parts[3]] if two else ffn_parts
    count = len(ffn_parts)
    gate_rows, up_rows = stack_rows(gate_up, swap(gate_up, 1, size))

    gate_part, up_part, inner = [], [], []
    for at in range(count):
        if at:
            ffn_parts[at], inner[-1] = tie(ffn_parts[at], inner[-1])
        if at == count - 1:
            ffn_parts[at], cot_flat = tie(ffn_parts[at], cot_flat)
        if two and at == 3:
            ffn_parts[3] = jnp.concatenate(ffn_parts[3])
        gate, up = mm(ffn_parts[at], gate_rows, NT), mm(ffn_parts[at], up_rows, NT)
        sig = jax.nn.sigmoid(gate)
        silu = gate * sig
        kept = tie(
            silu.astype(bf16),
            (up * sig * (1.0 + gate * (1.0 - sig))).astype(bf16),
            (silu * up).astype(bf16),
        )
        for held, one in zip((up_part, gate_part, inner), kept):
            held.append(one)
    inner[-1], down = tie(inner[-1], down)
    down_own, down_other = cross(inner, cot_flat)
    down_received, down_own = tie(swap(down, 1, size), down_own)
    down_other = swap(down_other, 1, size)
    down_pair = None
    (down_rows,) = stack_rows(down[None], down_received[None])
    cot_parts = [*cot_flat[:3], jnp.concatenate(cot_flat[3:])] if two else cot_flat
    gate_grad, up_grad, totals = [None] * count, [None] * count, []

    def ffn_part(at):
        nonlocal down_other, down_pair
        part = cot_parts[at]
        if len(totals) == 1:
            down_other, totals[0] = tie(down_other, totals[0])
            down_pair = add_pair(down_own, down_other)[0]
            part, down_pair = tie(part, down_pair)
        if totals:
            part, totals[-1] = tie(part, totals[-1])
        inner_grad = mm(part, down_rows, NT)
        gate_grad[at] = (inner_grad * gate_part[at].astype(f32)).astype(bf16)
        up_grad[at] = (inner_grad * up_part[at].astype(f32)).astype(bf16)
        totals.append(
            add(mm(gate_grad[at], gate_rows, NN), mm(up_grad[at], up_rows, NN)).astype(bf16)
        )
        return totals[-1]

    ffn_sum = Scatter(ffn_part, bits, size)
    ffn_down_grad = lax.psum_scatter(down_pair, "dp", scatter_dimension=0, tiled=True)
    if two:
        ffn_sum.own, gate_grad[0] = tie(ffn_sum.own, gate_grad[0])
    gate_own, gate_other = cross(gate_grad, ffn_flat)
    gate_other, up_grad[0] = tie(gate_other, up_grad[0])
    up_own, up_other = cross(up_grad, ffn_flat)
    up_other, ffn_down_grad = tie(up_other, ffn_down_grad)
    if two:
        ffn_sum.moved, up_other = tie(ffn_sum.moved, up_other)
        ffn_sum.finish()
    gate_up_pair = add_pair(gate_own, swap(gate_other, 1, size), 2, 0)
    gate_up_pair, up_own = tie(gate_up_pair, up_own)
    gate_up_pair = add_pair(up_own, swap(up_other, 1, size), 2, 1, gate_up_pair)
    ffn_in_grad = ffn_sum.total(resid)[0]
    gate_up_grad = lax.psum_scatter(gate_up_pair, "dp", scatter_dimension=1, tiled=True)

    scaled = ffn_in_grad * norm2_gain
    resid_grad = cot_own.astype(f32) + row_scale * (
        scaled - resid * row_scale * row_scale * jnp.mean(scaled * resid, axis=-1, keepdims=True)
    )
    norm2_part = jnp.sum(ffn_in_grad * resid * row_scale, axis=0)
    mixer_parts = gather_start(resid_grad.astype(bf16), bits, size)[1]
    output_parts = [mm(inner[at], down_rows, NN).astype(bf16) for at in range(count)]
    output_parts, mixer_parts[-1] = tie(output_parts, mixer_parts[-1])
    output_sum = Scatter(lambda at: output_parts[at], bits, size)
    mixer_grad = jnp.concatenate(mixer_parts)

    out_own, out_other = cross([gated], mixer_parts)
    mixer_grad, out_other = tie(mixer_grad, out_other)
    out_pair = add_pair(out_own, swap(out_other, 1, size))[0]
    gated_grad = mm(mixer_grad, out_weights, NT)
    proj_grad, floor_grad, gain_grad = recurrence_back(
        info, proj, floor_row, gain_row, seg, mixed, gated_grad, states, scores, half_heads, size
    )
    if two:
        output_sum.moved, proj_grad = tie(output_sum.moved, proj_grad)

    proj_grad, out_pair = tie(proj_grad, out_pair)
    proj_own, proj_other = cross(normed_parts, [proj_grad], by_rows=False)
    proj_other, proj_grad, gate_up_grad = tie(proj_other, proj_grad, gate_up_grad)
    normed_all = mm(proj_grad, proj_weights, NT).astype(bf16)
    proj_other, normed_all, floor_grad = tie(swap(proj_other, 1, size), normed_all, floor_grad)
    proj_pair = add_pair(proj_own, proj_other)[0]
    normed_sum = Scatter(lambda at: chunk(normed_all, at), bits, size)
    if two:
        normed_sum.finish()
    normed_grad = normed_sum.total(proj_own)[0]
    out_grad = lax.psum_scatter(out_pair, "dp", scatter_dimension=1, tiled=True)
    proj_pair, out_grad = tie(proj_pair, out_grad)
    proj_w_grad = lax.psum_scatter(proj_pair, "dp", scatter_dimension=0, tiled=True).astype(f32)

    input_scale = rms_scale(own_rows)
    scaled_in = normed_grad * norm1_gain
    input_grad = resid_grad + input_scale * (
        scaled_in
        - own_rows
        * input_scale
        * input_scale
        * jnp.mean(scaled_in * own_rows, axis=-1, keepdims=True)
    )
    norm1_part = jnp.sum(normed_grad * own_rows * input_scale, axis=0)
    input_grad = from_row(input_grad)

    if two:
        output_sum.finish()
        output_sum.sends, norm1_part = tie(output_sum.sends, norm1_part)
    output = from_row(add(resid, output_sum.total(resid)[0]).astype(bf16))

    vector_grads = jnp.concatenate((gain_grad, floor_grad))
    vector_grads = vector_grads[:, :half_width] + swap(vector_grads[:, half_width:], 1, size)
    moved = [
        lax.ppermute(vector_grads, "dp", [(at, (at + slot) % depth) for at in range(depth)])
        for slot in range(1, depth)
    ]
    vector_grads = sum(moved, vector_grads)
    vector_len = half_width // depth
    vector_grads = lax.dynamic_slice_in_dim(vector_grads, place * vector_len, vector_len, 1)
    norm_grads = jnp.stack((norm1_part, norm2_part))
    for bit in [1] + bits:
        norm_grads = norm_grads + swap(norm_grads, bit, size)
    moved = [
        lax.ppermute(norm_grads, "dp", [(at, (at + slot) % depth) for at in range(depth)])
        for slot in range(1, depth)
    ]
    stacked = jnp.stack([norm_grads] + moved)
    order = (place - jnp.arange(depth)) % depth
    norm_grads = jnp.sum(jnp.zeros_like(stacked).at[order].set(stacked), axis=0)

    return (
        output,
        input_grad,
        proj_w_grad[:, 0:half_width],
        proj_w_grad[:, half_width : 2 * half_width],
        proj_w_grad[:, 2 * half_width : 3 * half_width],
        proj_w_grad[:, 3 * half_width : 4 * half_width],
        out_grad.astype(f32),
        vector_grads[0],
        vector_grads[1],
        norm_grads[0],
        norm_grads[1],
        gate_up_grad[0].astype(f32).T,
        gate_up_grad[1].astype(f32).T,
        ffn_down_grad.astype(f32).T,
    )


def solution(mesh):
    placed = (
        P("dp", "head", None),
        P("dp", None),
        P(),
        P(None, "head"),
        P(None, "head"),
        P(None, "head"),
        P(None, "head"),
        P("head"),
        P("head"),
        P("head", None),
        P(),
        P(None, ("head", "dp")),
        P(None, ("head", "dp")),
        P(None, ("head", "dp")),
        P("dp", "head", None),
    )
    return jax.shard_map(
        functools.partial(per_device, mesh.shape["head"], mesh.shape["dp"]),
        mesh=mesh,
        in_specs=placed,
        out_specs=(
            P("dp", "head", None),
            P("dp", "head", None),
            P("dp", "head"),
            P("dp", "head"),
            P("dp", "head"),
            P("dp", "head"),
            P("head", "dp"),
            P(("head", "dp")),
            P(("head", "dp")),
            P(),
            P(),
            P(None, ("head", "dp")),
            P(None, ("head", "dp")),
            P(None, ("head", "dp")),
        ),
        check_vma=False,
    )
```
